128 devices in a mesh: row: 16 (over y_hi, x, core), col: 8 (over y_lo, z).
Axes of the slice: x: 4, y: 4 (y_hi: 2, y_lo: 2; y = y_hi * 2 + y_lo), z: 4, core: 2. Of those that a mesh axis runs over, the one named last changes fastest.
Arguments:
- blocks: float32 [4096, 24, 4096], P('row', 'col')
- columns: int32 [4096, 24], P('row', 'col'), may hold values from 0 to 4095, as said below
- counts: int32 [4096, 8], P('row', 'col'), may hold values from 0 to 3, as said below
- old_basis: float32 [128, 262144], P(None, 'row')
- vectors: float32 [16, 262144], P(None, 'row')
Outputs:
- new_block: float32 [16, 262144], P(None, 'row')
- coeffs: float32 [128, 16], replicated
- factor: float32 [16, 16], replicated
The draws below stay inside these ranges and needn't reach their ends.
Inputs may be any that keep to these rules, and one draw needn't show every extreme that they name: `columns`: slot k * 3 + s of a block row names a global block column g held by column group k, that is (g % 256) // (256 / the number of column groups) == k; slot 0 of the group holding the row's own block column names that column. The counts of one block row sum to 11; the group holding the row's own block column has 3.
All inputs are finite; a program needn't handle non-finite values.
Results may differ from the reference program's by a relative error of at most 0.0003.
Values sent between devices are 32-bit elements; how exact they have to be, the bound alone decides.
A program may use at most 192 MiB of HBM per device.

```python
import jax
import jax.numpy as jnp
from jax import lax

B = 64
S = 16
NBLK = 11
SLOT = 3
BR_DEV = 256
NB = 4096
NTOT = 262144
KS = 128
N_ROW = 16
N_COL = 8


def pattern(key):
    key = jax.random.fold_in(key, 100)
    score_key, index_key = jax.random.split(key)
    sub_width = BR_DEV // N_COL
    row_ids = jnp.arange(NB, dtype=jnp.int32)
    own_group = row_ids % BR_DEV // sub_width
    groups = jnp.arange(N_COL, dtype=jnp.int32)
    scores = jax.random.randint(score_key, (NB, N_COL), 0, 1 << 20) * N_COL + groups[None, :]
    scores = jnp.where(groups[None, :] == own_group[:, None], -1, scores)
    order = jnp.argsort(scores, axis=1)
    ranks = jnp.argsort(order, axis=1).astype(jnp.int32)
    count_table = jnp.clip(NBLK - SLOT * ranks, 0, SLOT)
    local_ids = jax.random.randint(index_key, (NB, N_COL, SLOT), 0, NB // N_COL)
    own_local = row_ids // BR_DEV * sub_width + row_ids % BR_DEV % sub_width
    first_slot = (groups[None, :, None] == own_group[:, None, None]) & (jnp.arange(SLOT, dtype=jnp.int32)[None, None, :] == 0)
    local_ids = jnp.where(first_slot, own_local[:, None, None], local_ids)
    global_ids = local_ids // sub_width * BR_DEV + groups[None, :, None] * sub_width + local_ids % sub_width
    return (count_table.astype(jnp.int32), global_ids.reshape(NB, N_COL * SLOT).astype(jnp.int32))


def basis_core(key):
    key = jax.random.fold_in(key, 200)
    period = B * B
    bit_count = int(period).bit_length() - 1
    picks = jax.random.permutation(jax.random.fold_in(key, 1), period)[:KS].astype(jnp.int32)
    cell_ids = jnp.arange(NTOT, dtype=jnp.int32) % period
    parity = jnp.zeros((KS, NTOT), jnp.int32)
    for position in range(bit_count):
        parity = parity ^ picks[:, None] >> position & 1 & (cell_ids[None, :] >> position & 1)
    signs = 2.0 * jax.random.bernoulli(jax.random.fold_in(key, 2), 0.5, (NTOT,)).astype(jnp.float32) - 1.0
    return (1.0 - 2.0 * parity.astype(jnp.float32)) * signs[None, :]


def draw_counts(key, part):
    shared = pattern(key)
    return shared[0]


def draw_columns(key, part):
    shared = pattern(key)
    return shared[1]


def draw_blocks(key, part):
    key = jax.random.fold_in(key, 5)
    values = jax.random.normal(key, (NB, N_COL * SLOT, B * B), jnp.float32)
    values = values / jnp.sqrt(jnp.float32(NBLK * B))
    row_ids = jnp.arange(NB, dtype=jnp.int32)
    own_slot = row_ids % BR_DEV // (BR_DEV // N_COL) * SLOT
    slot_hit = (jnp.arange(N_COL * SLOT, dtype=jnp.int32)[None, :] == own_slot[:, None]).astype(jnp.float32)
    identity = (jnp.arange(B * B, dtype=jnp.int32) % (B + 1) == 0).astype(jnp.float32)
    return values + slot_hit[:, :, None] * identity[None, None, :]


def draw_old_basis(key, part):
    core = basis_core(key)
    key = jax.random.fold_in(key, 3)
    drift = 0.1 * jax.random.normal(key, (KS, NTOT), jnp.float32)
    return core + drift


def draw_vectors(key, part):
    shared = basis_core(key)[KS - S:]
    key = jax.random.fold_in(key, 4)
    fresh_part = jax.random.normal(key, (S, NTOT), jnp.float32)
    return 0.7 * shared + 0.7 * fresh_part


def setup_inputs(seed: int = 0) -> dict:
    streams_of = jax.random.split(jax.random.key(seed), 6)
    return {
        "blocks": draw_blocks(jax.random.fold_in(streams_of[5], 71), 0),
        "columns": draw_columns(jax.random.fold_in(streams_of[5], 71), 0),
        "counts": draw_counts(jax.random.fold_in(streams_of[5], 71), 0),
        "old_basis": draw_old_basis(jax.random.fold_in(streams_of[5], 71), 0),
        "vectors": draw_vectors(jax.random.fold_in(streams_of[5], 71), 0),
    }


def matrix_product(blocks, columns, counts, vectors):
    vector_grid = vectors.reshape(S, NB, B)
    slot_ids = jnp.arange(N_COL * SLOT, dtype=jnp.int32) % SLOT

    def one_shard(items):
        shard_blocks, shard_columns, shard_counts = items
        live_mask = (slot_ids[None, :] < jnp.repeat(shard_counts, SLOT, axis=1)).astype(jnp.float32)
        taken = jnp.take(vector_grid, shard_columns.astype(jnp.int32), axis=1)
        block_mats = shard_blocks.reshape(BR_DEV, N_COL * SLOT, B, B)
        return jnp.einsum('nrsb,rsba->nra', taken * live_mask[None, :, :, None], block_mats, precision=lax.Precision.HIGHEST)
    stacked = lax.map(one_shard, (blocks.reshape(N_ROW, BR_DEV, N_COL * SLOT, B * B), columns.reshape(N_ROW, BR_DEV, N_COL * SLOT), counts.reshape(N_ROW, BR_DEV, N_COL)))
    return jnp.transpose(stacked, (1, 0, 2, 3)).reshape(S, NTOT)

def project(left, right):
    return jnp.dot(left.astype(jnp.float32), right.T.astype(jnp.float32), precision=lax.Precision.HIGHEST, preferred_element_type=jnp.float32)

def reference(blocks, columns, counts, old_basis, vectors):
    product = matrix_product(blocks, columns, counts, vectors)
    first_proj = project(old_basis, product) / NTOT
    once = product - jnp.dot(first_proj.T, old_basis, precision=lax.Precision.HIGHEST)
    second_proj = project(old_basis, once) / NTOT
    twice = once - jnp.dot(second_proj.T, old_basis, precision=lax.Precision.HIGHEST)
    gram = project(twice, twice) / NTOT
    factor = jnp.linalg.cholesky(gram)
    new_block = lax.linalg.triangular_solve(factor, twice, left_side=True, lower=True)
    return (new_block, first_proj + second_proj, factor)
```

```python
import functools

import jax
import jax.numpy as jnp
from jax import lax
from jax.experimental import pallas as pl
from jax.experimental.pallas import tpu as pltpu
from jax.sharding import PartitionSpec as P

f32 = jnp.float32
bf16 = jnp.bfloat16
MESH = pl.DeviceIdType.MESH

B = 64
S = 16
SLOT = 3
BAND = 8
ROWS = 256
PIECE = 2048
UNK = 16384
KS = 128
TOTAL = 262144
ZERO_BLOCK = 512


def split(x):
    hi = x.astype(bf16)
    return hi, (x - hi.astype(f32)).astype(bf16)


def stacked(x):
    hi, lo = split(x)
    return jnp.concatenate([hi, lo], 0)


def fold(x):
    return x[:S] + x[S:]


def wide(x):
    two = stacked(x)
    return jnp.concatenate([two, two], 1)


def dot(a, b):
    return jnp.dot(a, b, preferred_element_type=f32)


def dot_nt(a, b):
    return lax.dot_general(a, b, (((1,), (1,)), ((), ())), preferred_element_type=f32)


def kernel(
    columns, counts, blocks, vectors, basis,
    out, coeffs_out, factor_out,
    stage, weights, grid, expand, basis_stage, basis2, pieces, partial, arrived, product, twice, final,
    red_src, red_sib, red_row, red_col,
    load_sem, basis_sem, own_sem, out_sem,
    s1, r1, f1, s2, r2, s3, r3, sib_s, sib_r, row_s, row_r, col_s, col_r,
):
    row = lax.axis_index("row")
    col = lax.axis_index("col")
    yh, x, core = row // 8, row // 2 % 4, row % 2
    yl, z = col // 4, col % 4
    chip = yh * 4 + x
    sibling = (row + 1 - 2 * core, col)

    def row_peer(m):
        c = (yh + m // 4) % 2 * 4 + (x + m % 4) % 4
        return c, (c * 2 + core, col)

    def col_peer(m):
        k = (yl + m // 4) % 2 * 4 + (z + m % 4) % 4
        return k, (row, k)

    own_load = pltpu.make_async_copy(
        vectors.at[:, pl.ds(pl.multiple_of(col * PIECE, PIECE), PIECE)], pieces.at[row], own_sem
    )
    own_load.start()
    loads = []
    for s in range(SLOT):
        load = pltpu.make_async_copy(blocks.at[s], stage.at[s], load_sem.at[s])
        load.start()
        loads.append(load)

    def basis_load(c):
        return pltpu.make_async_copy(
            basis.at[:, pl.ds(c * PIECE, PIECE)], basis_stage.at[c % 2], basis_sem.at[c % 2]
        )

    basis_load(0).start()
    basis_load(1).start()

    barrier = pltpu.get_barrier_semaphore()
    peers = [sibling] + [row_peer(m)[1] for m in range(1, 8)] + [col_peer(m)[1] for m in range(1, 8)]
    for peer in peers:
        pl.semaphore_signal(barrier, inc=1, device_id=peer, device_id_type=MESH)
    pl.semaphore_wait(barrier, len(peers))

    own_load.wait()
    sends = []

    def send(src, dst, ssem, rsem, peer):
        copy = pltpu.make_async_remote_copy(src, dst, ssem, rsem, device_id=peer, device_id_type=MESH)
        copy.start()
        sends.append(copy)

    def arrival(dst, ssem, rsem):
        return pltpu.make_async_remote_copy(dst, dst, ssem, rsem, device_id=sibling, device_id_type=MESH)

    for m in (2, 6, 1, 3, 5, 7, 4):
        send(pieces.at[row], pieces.at[row], s1.at[m], r1.at[row], row_peer(m)[1])
    send(pieces.at[row], pieces.at[row], f1.at[0], r1.at[row], sibling)

    cell = lax.broadcasted_iota(jnp.int32, (128, 512), 0)
    spot = lax.broadcasted_iota(jnp.int32, (128, 512), 1)
    expand[...] = jnp.where(
        cell == spot // 256 * 64 + spot % 32 * 2 + spot // 128 % 2, 1.0, 0.0
    ).astype(bf16)
    grid[ZERO_BLOCK] = jnp.zeros((64, 128), bf16)

    for s in range(SLOT):
        loads[s].wait()

        @pl.loop(0, ROWS // BAND)
        def _(band, s=s):
            for i in range(BAND):
                hi, lo = split(stage[s, band, pl.ds(i, 32, stride=BAND), :])
                weights[band * BAND + i, 32 * s:32 * s + 32, :] = hi
                weights[band * BAND + i, 96 + 32 * s:128 + 32 * s, :] = lo

    own_basis = pl.multiple_of(col * 16, 16)
    gram_rows = jnp.zeros((2 * S, 2 * KS), f32)
    for c in range(8):
        basis_load(c).wait()
        chunk = stacked(basis_stage[c % 2])
        basis2[:, c * PIECE:(c + 1) * PIECE] = chunk
        if c + 2 < 8:
            basis_load(c + 2).start()
        left = jnp.concatenate(
            [
                basis2[pl.ds(own_basis, 16), c * PIECE:(c + 1) * PIECE],
                basis2[pl.ds(KS + own_basis, 16), c * PIECE:(c + 1) * PIECE],
            ],
            0,
        )
        gram_rows += dot_nt(left, chunk)

    def stage_sib(n, value):
        red_src[n, 0] = value
        send(red_src.at[n, 0], red_sib.at[n], sib_s.at[n], sib_r.at[n], sibling)

    def stage_row(n):
        arrival(red_sib.at[n], sib_s.at[n], sib_r.at[n]).wait_recv()
        red_row[n, chip] = red_src[n, 0] + red_sib[n]
        for m in range(1, 8):
            send(red_row.at[n, chip], red_row.at[n, chip], row_s.at[n, m], row_r.at[n, chip], row_peer(m)[1])

    def stage_col(n):
        for m in range(1, 8):
            c = row_peer(m)[0]
            arrival(red_row.at[n, c], row_s.at[n, m], row_r.at[n, c]).wait_recv()
        total = red_row[n, 0]
        for c in range(1, 8):
            total += red_row[n, c]
        red_col[n, col] = total * (1.0 / TOTAL)
        for m in range(1, 8):
            send(red_col.at[n, col], red_col.at[n, col], col_s.at[n, m], col_r.at[n, col], col_peer(m)[1])

    def stage_end(n):
        for m in range(1, 8):
            k = col_peer(m)[0]
            arrival(red_col.at[n, k], col_s.at[n, m], col_r.at[n, k]).wait_recv()

    def summed(n):
        total = red_col[n, 0]
        for k in range(1, 8):
            total += red_col[n, k]
        return total

    both = gram_rows[:, :KS] + gram_rows[:, KS:]
    stage_sib(0, fold(both))
    stage_row(0)

    def prepare(r):
        two = stacked(pieces[r])
        for h in range(4):
            left = jnp.concatenate([two[:, 128 * u:128 * u + 128] for u in range(4 * h, 4 * h + 4)], 0)
            spread = dot(left, expand[...]).astype(bf16)
            for u in range(4):
                for q in range(2):
                    for p in range(2):
                        lanes = (2 * q + p) * 128
                        grid[r * 32 + 2 * (4 * h + u) + q, 32 * p:32 * p + 32, :] = (
                            spread[32 * u:32 * u + 32, lanes:lanes + 128]
                        )

    prepare(row)
    order = (1, 3, 4, 2, 5, 7, 6)
    for n, m in enumerate(order):
        r = row_peer(m)[0] * 2 + core
        arrival(pieces.at[r], s1.at[m], r1.at[r]).wait_recv()
        send(pieces.at[r], pieces.at[r], f1.at[m], r1.at[r], sibling)
        prepare(r)
        q = row_peer(((0,) + order)[n])[0] * 2 + 1 - core
        arrival(pieces.at[q], f1.at[m], r1.at[q]).wait_recv()
        prepare(q)
    q = row_peer(order[-1])[0] * 2 + 1 - core
    arrival(pieces.at[q], f1.at[0], r1.at[q]).wait_recv()
    prepare(q)

    stage_col(0)

    low = lax.broadcasted_iota(jnp.int32, (S, 128), 1) < 64
    group = lax.broadcasted_iota(jnp.int32, (64, 128), 1) // 32

    def block_row(i):
        live = counts[0, i]
        where = []
        for t in range(SLOT):
            g = columns[t, i]
            where.append(jnp.where(live > t, g // ROWS * 32 + g % 32, ZERO_BLOCK))
        v0, v1, v2 = [grid[w] for w in where]
        first = jnp.where(group == 1, v1, jnp.where(group == 2, v2, v0))
        second = jnp.where(group == 0, v1, v2)
        left = jnp.concatenate([first, second], 1)[:, :192]
        res = dot(left, weights[i])
        return res[0:16] + res[16:32], res[32:48] + res[48:64]

    def piece(n, proj):
        m = 7 - n
        d = (yl + m // 4) % 2 * 4 + (z + m % 4) % 4
        for u in range(16):
            even0, odd0 = block_row(d * 32 + 2 * u)
            even1, odd1 = block_row(d * 32 + 2 * u + 1)
            partial[d, :, 128 * u:128 * u + 128] = jnp.where(low, even0, odd1) + pltpu.roll(
                jnp.where(low, even1, odd0), 64, 1
            )

        @pl.when(m > 0)
        def _():
            pltpu.make_async_remote_copy(
                partial.at[d], arrived.at[col], s2.at[m], r2.at[col], device_id=(row, d), device_id_type=MESH
            ).start()

        chunk = basis2[:, pl.ds(pl.multiple_of(d * PIECE, PIECE), PIECE)]
        return proj + dot_nt(stacked(partial[d]), chunk)

    proj = lax.fori_loop(0, 8, piece, jnp.zeros((2 * S, 2 * KS), f32))
    both = proj[:, :KS] + proj[:, KS:]
    stage_sib(1, fold(both))
    stage_row(1)
    stage_end(0)
    stage_col(1)

    total = partial[col]
    for m in range(1, 8):
        k = col_peer(m)[0]
        arrival(arrived.at[k], s2.at[m], r2.at[k]).wait_recv()
    for m in range(1, 8):
        total += arrived[col_peer(m)[0]]
    product[col] = total
    for m in (6, 2, 5, 7, 1, 3, 4):
        send(product.at[col], product.at[col], s3.at[m], r3.at[col], col_peer(m)[1])

    stage_end(1)
    first_proj = summed(1)
    basis_gram = jnp.concatenate([red_col[0, k] for k in range(8)], 0)
    coeffs = 2.0 * first_proj - jnp.dot(
        first_proj, basis_gram, precision=lax.Precision.HIGHEST, preferred_element_type=f32
    )
    coeffs_out[...] = coeffs
    coeffs2 = wide(coeffs)

    def remove(k):
        chunk = basis2[:, pl.ds(pl.multiple_of(k * PIECE, PIECE), PIECE)]
        rest = stacked(product[k] - fold(dot(coeffs2, chunk)))
        twice[k] = rest
        return rest

    own_rest = remove(col)
    quads = dot_nt(own_rest, own_rest)
    quads = quads[:, :S] + quads[:, S:]
    stage_sib(2, jnp.concatenate([fold(quads), jnp.zeros((S, 128 - S), f32)], 1))
    stage_row(2)
    stage_col(2)
    for m in (1, 3, 4, 2, 5, 7, 6):
        k = col_peer(m)[0]
        arrival(product.at[k], s3.at[m], r3.at[k]).wait_recv()
        remove(k)
    stage_end(2)

    lane = lax.broadcasted_iota(jnp.int32, (S, 128), 1)
    line = lax.broadcasted_iota(jnp.int32, (S, 128), 0)
    work = jnp.where(lane == line + S, 1.0, summed(2))
    factor = jnp.zeros((S, 128), f32)
    scale = jnp.zeros((S, 128), f32)
    for j in range(S):
        column = jnp.broadcast_to(work[:, j:j + 1], (S, 128))
        pivot = jnp.broadcast_to(column[j:j + 1, :], (S, 128))
        root = lax.rsqrt(pivot)
        factor = jnp.where((lane == j) & (line >= j), column * root, factor)
        scale = jnp.where(line == j, root, scale)
        ratio = jnp.where(line > j, column / pivot, 0.0)
        work = work - ratio * jnp.broadcast_to(work[j:j + 1, :], (S, 128))
    factor_out[...] = factor[:, :S]
    inverse = (work * scale)[:, S:2 * S]
    inverse2 = wide(inverse)
    writes = []
    for k in range(8):
        final[k] = fold(dot(inverse2, twice[k]))
        write = pltpu.make_async_copy(final.at[k], out.at[:, pl.ds(k * PIECE, PIECE)], out_sem.at[k])
        write.start()
        writes.append(write)

    for copy in sends:
        copy.wait_send()
    for m in range(1, 8):
        arrival(partial.at[col_peer(m)[0]], s2.at[m], r2.at[col]).wait_send()
    for write in writes:
        write.wait()


def body(blocks, columns, counts, old_basis, vectors):
    bands = blocks.reshape(ROWS // BAND, BAND, SLOT, 32, 128).transpose(2, 0, 3, 1, 4)
    bands = bands.reshape(SLOT, ROWS // BAND, 32 * BAND, 128)
    D = pltpu.SemaphoreType.DMA
    V = pltpu.VMEM
    any_space = pl.BlockSpec(memory_space=pl.ANY)
    smem = pl.BlockSpec(memory_space=pltpu.SMEM)
    vmem = pl.BlockSpec(memory_space=pltpu.VMEM)
    new_block, coeffs, factor = pl.pallas_call(
        kernel,
        out_shape=(
            jax.ShapeDtypeStruct((S, UNK), f32),
            jax.ShapeDtypeStruct((S, KS), f32),
            jax.ShapeDtypeStruct((S, S), f32),
        ),
        in_specs=[smem, smem, any_space, any_space, any_space],
        out_specs=(any_space, vmem, vmem),
        scratch_shapes=[
            V((SLOT, ROWS // BAND, 32 * BAND, 128), f32),
            V((ROWS, 192, 128), bf16),
            V((ZERO_BLOCK + 1, 64, 128), bf16),
            V((128, 512), bf16),
            V((2, KS, PIECE), f32),
            V((2 * KS, UNK), bf16),
            V((16, S, PIECE), f32),
            V((8, S, PIECE), f32),
            V((8, S, PIECE), f32),
            V((8, S, PIECE), f32),
            V((8, 2 * S, PIECE), bf16),
            V((8, S, PIECE), f32),
            V((3, 1, S, 128), f32),
            V((3, S, 128), f32),
            V((3, 8, S, 128), f32),
            V((3, 8, S, 128), f32),
            D((SLOT,)), D((2,)), D, D((8,)),
            D((8,)), D((16,)), D((8,)), D((8,)), D((8,)), D((8,)), D((8,)),
            D((3,)), D((3,)), D((3, 8)), D((3, 8)), D((3, 8)), D((3, 8)),
        ],
        compiler_params=pltpu.CompilerParams(
            collective_id=0, has_side_effects=True, vmem_limit_bytes=62 << 20
        ),
    )(columns.T, counts.T, bands, vectors, old_basis)
    return new_block, coeffs.T, factor


def solution(mesh):
    return jax.shard_map(
        body,
        mesh=mesh,
        in_specs=(
            P("row", "col", None),
            P("row", "col"),
            P("row", "col"),
            P(None, "row"),
            P(None, "row"),
        ),
        out_specs=(P(None, "row"), P(), P()),
        check_vma=False,
    )
```

```python
import functools

import jax
import jax.numpy as jnp
from jax import lax
from jax.experimental import pallas as pl
from jax.experimental.pallas import tpu as pltpu
from jax.sharding import PartitionSpec as P

f32 = jnp.float32
bf16 = jnp.bfloat16
MESH = pl.DeviceIdType.MESH

B = 64
S = 16
SLOT = 3
BAND = 8
ROWS = 256
PIECE = 2048
UNK = 16384
KS = 128
TOTAL = 262144
ZERO_BLOCK = 512


def split(x):
    hi = x.astype(bf16)
    return hi, (x - hi.astype(f32)).astype(bf16)


def stacked(x):
    hi, lo = split(x)
    return jnp.concatenate([hi, lo], 0)


def fold(x):
    return x[:S] + x[S:]


def wide(x):
    two = stacked(x)
    return jnp.concatenate([two, two], 1)


def dot(a, b):
    return jnp.dot(a, b, preferred_element_type=f32)


def dot_nt(a, b):
    return lax.dot_general(a, b, (((1,), (1,)), ((), ())), preferred_element_type=f32)


def kernel(
    columns, counts, blocks, vectors, basis,
    twice_out, coeffs_out, factor_out, inverse_out,
    stage, weights, grid, expand, basis_stage, basis2, pieces, partial, arrived, product, twice,
    red_src, red_sib, red_row, red_col,
    load_sem, basis_sem, own_sem, out_sem,
    s1, r1, s2, r2, s3, r3, sib_s, sib_r, row_s, row_r, col_s, col_r,
):
    row = lax.axis_index("row")
    col = lax.axis_index("col")
    yh, x, core = row // 8, row // 2 % 4, row % 2
    yl, z = col // 4, col % 4
    chip = yh * 4 + x
    sibling = (row + 1 - 2 * core, col)

    def row_peer(m):
        c = (yh + m // 4) % 2 * 4 + (x + m % 4) % 4
        return c, (c * 2 + core, col)

    def col_peer(m):
        k = (yl + m // 4) % 2 * 4 + (z + m % 4) % 4
        return k, (row, k)

    own_loads = []
    for h in range(2):
        own_loads.append(
            pltpu.make_async_copy(
                vectors.at[8 * h:8 * h + 8, pl.ds(pl.multiple_of(col * PIECE, PIECE), PIECE)],
                pieces.at[h, row],
                own_sem.at[h],
            )
        )
        own_loads[h].start()
    loads = []
    for s in range(SLOT):
        load = pltpu.make_async_copy(blocks.at[s], stage.at[s], load_sem.at[s])
        load.start()
        loads.append(load)

    def basis_load(c):
        return pltpu.make_async_copy(
            basis.at[:, pl.ds(c * PIECE, PIECE)], basis_stage.at[c % 2], basis_sem.at[c % 2]
        )

    basis_load(0).start()
    basis_load(1).start()

    barrier = pltpu.get_barrier_semaphore()
    peers = [sibling] + [row_peer(m)[1] for m in range(1, 8)] + [col_peer(m)[1] for m in range(1, 8)]
    for peer in peers:
        pl.semaphore_signal(barrier, inc=1, device_id=peer, device_id_type=MESH)

    cell = lax.broadcasted_iota(jnp.int32, (128, 512), 0)
    spot = lax.broadcasted_iota(jnp.int32, (128, 512), 1)
    expand[...] = jnp.where(
        cell == spot // 256 * 64 + spot % 32 * 2 + spot // 128 % 2, 1.0, 0.0
    ).astype(bf16)
    grid[ZERO_BLOCK] = jnp.zeros((64, 128), bf16)

    for s in range(SLOT):
        loads[s].wait()

        @pl.loop(0, ROWS // BAND)
        def _(band, s=s):
            for i in range(BAND):
                hi, lo = split(stage[s, band, pl.ds(i, 32, stride=BAND), :])
                weights[band * BAND + i, 32 * s:32 * s + 32, :] = hi
                weights[band * BAND + i, 96 + 32 * s:128 + 32 * s, :] = lo

    pl.semaphore_wait(barrier, len(peers))

    sends = []

    def send(src, dst, ssem, rsem, peer):
        copy = pltpu.make_async_remote_copy(src, dst, ssem, rsem, device_id=peer, device_id_type=MESH)
        copy.start()
        sends.append(copy)

    def arrival(dst, ssem, rsem):
        return pltpu.make_async_remote_copy(dst, dst, ssem, rsem, device_id=sibling, device_id_type=MESH)

    def pass_on(h, r, n, peer):
        send(pieces.at[h, r], pieces.at[h, r], s1.at[h, n], r1.at[h, r], peer)

    for h in range(2):
        own_loads[h].wait()
        for m in (4, 2):
            pass_on(h, row, m, row_peer(m)[1])
    for h in range(2):
        for m in (1, 3):
            pass_on(h, row, m, row_peer(m)[1])
        pass_on(h, row, 0, sibling)

    def take(h, m):
        r = row_peer(m)[0] * 2 + core
        arrival(pieces.at[h, r], s1.at[h, 0], r1.at[h, r]).wait_recv()
        if m == 4:
            pass_on(h, r, 8, row_peer(1)[1])
            pass_on(h, r, 9, row_peer(3)[1])
        if m == 2:
            pass_on(h, r, 10, row_peer(4)[1])
        pass_on(h, r, 10 + m, sibling)

    def take_sibling(h, m):
        r = row_peer(m)[0] * 2 + 1 - core
        arrival(pieces.at[h, r], s1.at[h, 0], r1.at[h, r]).wait_recv()

    own_basis = pl.multiple_of(col * 16, 16)
    gram_rows = jnp.zeros((2 * S, 2 * KS), f32)
    for c in range(8):
        basis_load(c).wait()
        chunk = stacked(basis_stage[c % 2])
        basis2[:, c * PIECE:(c + 1) * PIECE] = chunk
        if c + 2 < 8:
            basis_load(c + 2).start()
        left = jnp.concatenate(
            [
                basis2[pl.ds(own_basis, 16), c * PIECE:(c + 1) * PIECE],
                basis2[pl.ds(KS + own_basis, 16), c * PIECE:(c + 1) * PIECE],
            ],
            0,
        )
        gram_rows += dot_nt(left, chunk)

    def stage_sib(n, value):
        red_src[n, 0] = value
        send(red_src.at[n, 0], red_sib.at[n], sib_s.at[n], sib_r.at[n], sibling)

    def stage_row(n):
        arrival(red_sib.at[n], sib_s.at[n], sib_r.at[n]).wait_recv()
        red_row[n, chip] = red_src[n, 0] + red_sib[n]
        for m in range(1, 8):
            send(red_row.at[n, chip], red_row.at[n, chip], row_s.at[n, m], row_r.at[n, chip], row_peer(m)[1])

    def stage_col(n):
        for m in range(1, 8):
            c = row_peer(m)[0]
            arrival(red_row.at[n, c], row_s.at[n, m], row_r.at[n, c]).wait_recv()
        total = red_row[n, 0]
        for c in range(1, 8):
            total += red_row[n, c]
        red_col[n, col] = total * (1.0 / TOTAL)
        for m in range(1, 8):
            send(red_col.at[n, col], red_col.at[n, col], col_s.at[n, m], col_r.at[n, col], col_peer(m)[1])

    def stage_end(n):
        for m in range(1, 8):
            k = col_peer(m)[0]
            arrival(red_col.at[n, k], col_s.at[n, m], col_r.at[n, k]).wait_recv()

    def summed(n):
        total = red_col[n, 0]
        for k in range(1, 8):
            total += red_col[n, k]
        return total

    both = gram_rows[:, :KS] + gram_rows[:, KS:]
    stage_sib(0, fold(both))
    stage_row(0)

    def prepare(r):
        two = stacked(jnp.concatenate([pieces[0, r], pieces[1, r]], 0))
        for h in range(4):
            left = jnp.concatenate([two[:, 128 * u:128 * u + 128] for u in range(4 * h, 4 * h + 4)], 0)
            spread = dot(left, expand[...]).astype(bf16)
            for u in range(4):
                for q in range(2):
                    for p in range(2):
                        lanes = (2 * q + p) * 128
                        grid[r * 32 + 2 * (4 * h + u) + q, 32 * p:32 * p + 32, :] = (
                            spread[32 * u:32 * u + 32, lanes:lanes + 128]
                        )

    for h in range(2):
        for m in (4, 2, 1, 3):
            take(h, m)
    for h in range(2):
        take_sibling(h, 0)
    prepare(row)
    prepare(row + 1 - 2 * core)
    for m in (4, 2, 1, 3):
        prepare(row_peer(m)[0] * 2 + core)
    for m in (5, 7, 6):
        take(0, m)
    for m in (4, 2, 1, 3):
        for h in range(2):
            take_sibling(h, m)
        prepare(row_peer(m)[0] * 2 + 1 - core)
    for m in (5, 7, 6):
        take(1, m)
        prepare(row_peer(m)[0] * 2 + core)
    for m in (5, 7, 6):
        for h in range(2):
            take_sibling(h, m)
        prepare(row_peer(m)[0] * 2 + 1 - core)

    stage_col(0)

    low = lax.broadcasted_iota(jnp.int32, (S, 128), 1) < 64
    group = lax.broadcasted_iota(jnp.int32, (64, 128), 1) // 32

    def block_row(i):
        live = counts[0, i]
        where = []
        for t in range(SLOT):
            g = columns[t, i]
            high = lax.shift_left(lax.shift_right_logical(g, 8), 5)
            where.append(jnp.where(live > t, high + jnp.bitwise_and(g, 31), ZERO_BLOCK))
        v0, v1, v2 = [grid[w] for w in where]
        first = jnp.where(group == 1, v1, jnp.where(group == 2, v2, v0))
        second = jnp.where(group == 0, v1, v2)
        left = jnp.concatenate([first, second], 1)[:, :192]
        res = dot(left, weights[i])
        return res[0:16] + res[16:32], res[32:48] + res[48:64]

    def piece(n, proj):
        m = n * 0
        for place, peer in enumerate((6, 5, 2, 7, 1, 4, 3)):
            m = jnp.where(n == place, peer, m)
        d = (yl + m // 4) % 2 * 4 + (z + m % 4) % 4
        for u in range(16):
            even0, odd0 = block_row(d * 32 + 2 * u)
            even1, odd1 = block_row(d * 32 + 2 * u + 1)
            partial[d, :, 128 * u:128 * u + 128] = jnp.where(low, even0, odd1) + pltpu.roll(
                jnp.where(low, even1, odd0), 64, 1
            )

        @pl.when(m > 0)
        def _():
            pltpu.make_async_remote_copy(
                partial.at[d], arrived.at[col], s2.at[m], r2.at[col], device_id=(row, d), device_id_type=MESH
            ).start()

        chunk = basis2[:, pl.ds(pl.multiple_of(d * PIECE, PIECE), PIECE)]
        return proj + dot_nt(stacked(partial[d]), chunk)

    proj = lax.fori_loop(0, 8, piece, jnp.zeros((2 * S, 2 * KS), f32))
    both = proj[:, :KS] + proj[:, KS:]
    stage_sib(1, fold(both))
    stage_row(1)
    stage_end(0)
    stage_col(1)

    total = partial[col]
    for m in range(1, 8):
        k = col_peer(m)[0]
        arrival(arrived.at[k], s2.at[m], r2.at[k]).wait_recv()
    for m in range(1, 8):
        total += arrived[col_peer(m)[0]]
    product[col] = total
    for m in (6, 2, 5, 7, 1, 3, 4):
        send(product.at[col], product.at[col], s3.at[m], r3.at[col], col_peer(m)[1])

    stage_end(1)
    first_proj = summed(1)
    basis_gram = jnp.concatenate([red_col[0, k] for k in range(8)], 0)
    coeffs = 2.0 * first_proj - jnp.dot(
        first_proj, basis_gram, precision=lax.Precision.HIGHEST, preferred_element_type=f32
    )
    coeffs_out[...] = coeffs
    coeffs2 = wide(coeffs)
    writes = []

    def seen(k):
        chunk = basis2[:, pl.ds(pl.multiple_of(k * PIECE, PIECE), PIECE)]
        return fold(dot(coeffs2, chunk))

    def keep(k, rest):
        rest = stacked(rest)
        twice[k] = rest
        write = pltpu.make_async_copy(twice.at[k], twice_out.at[k], out_sem.at[k])
        write.start()
        writes.append(write)
        return rest

    def remove(m):
        k = col_peer(m)[0]
        arrival(product.at[k], s3.at[m], r3.at[k]).wait_recv()
        keep(k, product[k] - arrived[k])

    def foresee(*ms):
        for m in ms:
            arrived[col_peer(m)[0]] = seen(col_peer(m)[0])

    own_rest = keep(col, product[col] - seen(col))
    quads = dot_nt(own_rest, own_rest)
    quads = quads[:, :S] + quads[:, S:]
    stage_sib(2, jnp.concatenate([fold(quads), jnp.zeros((S, 128 - S), f32)], 1))
    foresee(1, 3)
    stage_row(2)
    foresee(4, 5, 7)
    stage_col(2)
    foresee(2, 6)
    for m in (1, 3, 4):
        remove(m)
    stage_end(2)

    lane = lax.broadcasted_iota(jnp.int32, (S, 128), 1)
    line = lax.broadcasted_iota(jnp.int32, (S, 128), 0)
    work = jnp.where(lane == line + S, 1.0, summed(2))
    factor = jnp.zeros((S, 128), f32)
    scale = jnp.zeros((S, 128), f32)
    for j in range(S):
        column = jnp.broadcast_to(work[:, j:j + 1], (S, 128))
        pivot = jnp.broadcast_to(column[j:j + 1, :], (S, 128))
        root = lax.rsqrt(pivot)
        factor = jnp.where((lane == j) & (line >= j), column * root, factor)
        scale = jnp.where(line == j, root, scale)
        ratio = jnp.where(line > j, column / pivot, 0.0)
        work = work - ratio * jnp.broadcast_to(work[j:j + 1, :], (S, 128))
    factor_out[...] = factor[:, :S]
    inverse_out[...] = work * scale

    for m in (5, 7, 2, 6):
        remove(m)

    for copy in sends:
        copy.wait_send()
    for m in range(1, 8):
        arrival(partial.at[col_peer(m)[0]], s2.at[m], r2.at[col]).wait_send()
    for write in writes:
        write.wait()


def finish(twice_in, coeffs_in, factor_in, inverse_in, out, coeffs_out, factor_out, twice, final, in_sem, out_sem, small_sem):
    loads, writes = [], []
    for k in range(8):
        loads.append(pltpu.make_async_copy(twice_in.at[k], twice.at[k], in_sem.at[k]))
    writes.append(pltpu.make_async_copy(coeffs_in, coeffs_out, small_sem.at[0]))
    writes.append(pltpu.make_async_copy(factor_in, factor_out, small_sem.at[1]))
    for copy in loads + writes:
        copy.start()
    inverse2 = wide(inverse_in[...][:, S:2 * S])
    for k in range(8):
        loads[k].wait()
        final[k] = fold(dot(inverse2, twice[k]))
        write = pltpu.make_async_copy(final.at[k], out.at[:, pl.ds(k * PIECE, PIECE)], out_sem.at[k])
        write.start()
        writes.append(write)
    for write in writes:
        write.wait()


def body(blocks, columns, counts, old_basis, vectors):
    bands = blocks.reshape(ROWS // BAND, BAND, SLOT, 32, 128).transpose(2, 0, 3, 1, 4)
    bands = bands.reshape(SLOT, ROWS // BAND, 32 * BAND, 128)
    D = pltpu.SemaphoreType.DMA
    V = pltpu.VMEM
    any_space = pl.BlockSpec(memory_space=pl.ANY)
    smem = pl.BlockSpec(memory_space=pltpu.SMEM)
    vmem = pl.BlockSpec(memory_space=pltpu.VMEM)
    twice, coeffs, factor, inverse = pl.pallas_call(
        kernel,
        out_shape=(
            jax.ShapeDtypeStruct((8, 2 * S, PIECE), bf16),
            jax.ShapeDtypeStruct((S, KS), f32),
            jax.ShapeDtypeStruct((S, S), f32),
            jax.ShapeDtypeStruct((S, 128), f32),
        ),
        in_specs=[smem, smem, any_space, any_space, any_space],
        out_specs=(any_space, vmem, vmem, vmem),
        scratch_shapes=[
            V((SLOT, ROWS // BAND, 32 * BAND, 128), f32),
            V((ROWS, 192, 128), bf16),
            V((ZERO_BLOCK + 1, 64, 128), bf16),
            V((128, 512), bf16),
            V((2, KS, PIECE), f32),
            V((2 * KS, UNK), bf16),
            V((2, 16, S // 2, PIECE), f32),
            V((8, S, PIECE), f32),
            V((8, S, PIECE), f32),
            V((8, S, PIECE), f32),
            V((8, 2 * S, PIECE), bf16),
            V((3, 1, S, 128), f32),
            V((3, S, 128), f32),
            V((3, 8, S, 128), f32),
            V((3, 8, S, 128), f32),
            D((SLOT,)), D((2,)), D((2,)), D((8,)),
            D((2, 18)), D((2, 16)), D((8,)), D((8,)), D((8,)), D((8,)),
            D((3,)), D((3,)), D((3, 8)), D((3, 8)), D((3, 8)), D((3, 8)),
        ],
        compiler_params=pltpu.CompilerParams(
            collective_id=0, has_side_effects=True, vmem_limit_bytes=62 << 20
        ),
    )(columns.T, counts.T, bands, vectors, old_basis)
    new_block, coeffs, factor = pl.pallas_call(
        finish,
        out_shape=(
            jax.ShapeDtypeStruct((S, UNK), f32),
            jax.ShapeDtypeStruct((S, KS), f32),
            jax.ShapeDtypeStruct((S, S), f32),
        ),
        in_specs=[any_space, any_space, any_space, vmem],
        out_specs=(any_space, any_space, any_space),
        scratch_shapes=[V((8, 2 * S, PIECE), bf16), V((8, S, PIECE), f32), D((8,)), D((8,)), D((2,))],
        compiler_params=pltpu.CompilerParams(vmem_limit_bytes=62 << 20),
    )(twice, coeffs, factor, inverse)
    return new_block, coeffs.T, factor


def solution(mesh):
    return jax.shard_map(
        body,
        mesh=mesh,
        in_specs=(
            P("row", "col", None),
            P("row", "col"),
            P("row", "col"),
            P(None, "row"),
            P(None, "row"),
        ),
        out_specs=(P(None, "row"), P(), P()),
        check_vma=False,
    )
```

```python
import functools

import jax
import jax.numpy as jnp
from jax import lax
from jax.experimental import pallas as pl
from jax.experimental.pallas import tpu as pltpu
from jax.sharding import PartitionSpec as P

f32 = jnp.float32
bf16 = jnp.bfloat16
MESH = pl.DeviceIdType.MESH

B = 64
S = 16
SLOT = 3
BAND = 8
ROWS = 256
PIECE = 2048
UNK = 16384
KS = 128
TOTAL = 262144
ZERO_BLOCK = 512


def split(x):
    hi = x.astype(bf16)
    return hi, (x - hi.astype(f32)).astype(bf16)


def stacked(x):
    hi, lo = split(x)
    return jnp.concatenate([hi, lo], 0)


def fold(x):
    return x[:S] + x[S:]


def wide(x):
    two = stacked(x)
    return jnp.concatenate([two, two], 1)


def dot(a, b):
    return jnp.dot(a, b, preferred_element_type=f32)


def dot_nt(a, b):
    return lax.dot_general(a, b, (((1,), (1,)), ((), ())), preferred_element_type=f32)


def kernel(
    columns, counts, blocks, vectors, basis,
    twice_out, coeffs_out, factor_out, inverse_out,
    stage, weights, grid, expand, basis_stage, basis2, pieces, partial, inbox, relay, foreseen, product, twice,
    red_src, red_sib, red_row, red_col,
    load_sem, basis_sem, own_sem, out_sem,
    s1, r1, s2, r2, s3, r3, sib_s, sib_r, row_s, row_r, col_s, col_r,
):
    row = lax.axis_index("row")
    col = lax.axis_index("col")
    yh, x, core = row // 8, row // 2 % 4, row % 2
    yl, z = col // 4, col % 4
    chip = yh * 4 + x
    sibling = (row + 1 - 2 * core, col)

    def row_peer(m):
        c = (yh + m // 4) % 2 * 4 + (x + m % 4) % 4
        return c, (c * 2 + core, col)

    def col_peer(m):
        k = (yl + m // 4) % 2 * 4 + (z + m % 4) % 4
        return k, (row, k)

    own_loads = []
    for h in range(2):
        own_loads.append(
            pltpu.make_async_copy(
                vectors.at[8 * h:8 * h + 8, pl.ds(pl.multiple_of(col * PIECE, PIECE), PIECE)],
                pieces.at[h, row],
                own_sem.at[h],
            )
        )
        own_loads[h].start()
    loads = []
    for s in range(SLOT):
        load = pltpu.make_async_copy(blocks.at[s], stage.at[s], load_sem.at[s])
        load.start()
        loads.append(load)

    def basis_load(c):
        return pltpu.make_async_copy(
            basis.at[:, pl.ds(c * PIECE, PIECE)], basis_stage.at[c % 2], basis_sem.at[c % 2]
        )

    basis_load(0).start()
    basis_load(1).start()

    barrier = pltpu.get_barrier_semaphore()
    peers = [sibling] + [row_peer(m)[1] for m in range(1, 8)] + [col_peer(m)[1] for m in range(1, 8)]
    for peer in peers:
        pl.semaphore_signal(barrier, inc=1, device_id=peer, device_id_type=MESH)

    cell = lax.broadcasted_iota(jnp.int32, (128, 512), 0)
    spot = lax.broadcasted_iota(jnp.int32, (128, 512), 1)
    expand[...] = jnp.where(
        cell == spot // 256 * 64 + spot % 32 * 2 + spot // 128 % 2, 1.0, 0.0
    ).astype(bf16)
    grid[ZERO_BLOCK] = jnp.zeros((64, 128), bf16)

    for s in range(SLOT):
        loads[s].wait()

        @pl.loop(0, ROWS // BAND)
        def _(band, s=s):
            for i in range(BAND):
                hi, lo = split(stage[s, band, pl.ds(i, 32, stride=BAND), :])
                weights[band * BAND + i, 32 * s:32 * s + 32, :] = hi
                weights[band * BAND + i, 96 + 32 * s:128 + 32 * s, :] = lo

    pl.semaphore_wait(barrier, len(peers))

    sends = []

    def send(src, dst, ssem, rsem, peer):
        copy = pltpu.make_async_remote_copy(src, dst, ssem, rsem, device_id=peer, device_id_type=MESH)
        copy.start()
        sends.append(copy)

    def arrival(dst, ssem, rsem):
        return pltpu.make_async_remote_copy(dst, dst, ssem, rsem, device_id=sibling, device_id_type=MESH)

    def pass_on(h, r, n, peer):
        send(pieces.at[h, r], pieces.at[h, r], s1.at[h, n], r1.at[h, r], peer)

    for h in range(2):
        own_loads[h].wait()
        for m in (4, 2):
            pass_on(h, row, m, row_peer(m)[1])
    for h in range(2):
        for m in (1, 3):
            pass_on(h, row, m, row_peer(m)[1])
        pass_on(h, row, 0, sibling)

    def take(h, m):
        r = row_peer(m)[0] * 2 + core
        arrival(pieces.at[h, r], s1.at[h, 0], r1.at[h, r]).wait_recv()
        if m == 4:
            pass_on(h, r, 8, row_peer(1)[1])
            pass_on(h, r, 9, row_peer(3)[1])
        if m == 2:
            pass_on(h, r, 10, row_peer(4)[1])
        pass_on(h, r, 10 + m, sibling)

    def take_sibling(h, m):
        r = row_peer(m)[0] * 2 + 1 - core
        arrival(pieces.at[h, r], s1.at[h, 0], r1.at[h, r]).wait_recv()

    own_basis = pl.multiple_of(col * 16, 16)
    gram_rows = jnp.zeros((2 * S, 2 * KS), f32)
    for c in range(8):
        basis_load(c).wait()
        chunk = stacked(basis_stage[c % 2])
        basis2[:, c * PIECE:(c + 1) * PIECE] = chunk
        if c + 2 < 8:
            basis_load(c + 2).start()
        left = jnp.concatenate(
            [
                basis2[pl.ds(own_basis, 16), c * PIECE:(c + 1) * PIECE],
                basis2[pl.ds(KS + own_basis, 16), c * PIECE:(c + 1) * PIECE],
            ],
            0,
        )
        gram_rows += dot_nt(left, chunk)

    def stage_sib(n, value):
        red_src[n, 0] = value
        send(red_src.at[n, 0], red_sib.at[n], sib_s.at[n], sib_r.at[n], sibling)

    def stage_row(n):
        arrival(red_sib.at[n], sib_s.at[n], sib_r.at[n]).wait_recv()
        red_row[n, chip] = red_src[n, 0] + red_sib[n]
        for m in range(1, 8):
            send(red_row.at[n, chip], red_row.at[n, chip], row_s.at[n, m], row_r.at[n, chip], row_peer(m)[1])

    def stage_col(n):
        for m in range(1, 8):
            c = row_peer(m)[0]
            arrival(red_row.at[n, c], row_s.at[n, m], row_r.at[n, c]).wait_recv()
        total = red_row[n, 0]
        for c in range(1, 8):
            total += red_row[n, c]
        red_col[n, col] = total * (1.0 / TOTAL)
        for m in range(1, 8):
            send(red_col.at[n, col], red_col.at[n, col], col_s.at[n, m], col_r.at[n, col], col_peer(m)[1])

    def stage_end(n):
        for m in range(1, 8):
            k = col_peer(m)[0]
            arrival(red_col.at[n, k], col_s.at[n, m], col_r.at[n, k]).wait_recv()

    def summed(n):
        total = red_col[n, 0]
        for k in range(1, 8):
            total += red_col[n, k]
        return total

    both = gram_rows[:, :KS] + gram_rows[:, KS:]
    stage_sib(0, fold(both))
    stage_row(0)

    def prepare(r):
        two = stacked(jnp.concatenate([pieces[0, r], pieces[1, r]], 0))
        for h in range(4):
            left = jnp.concatenate([two[:, 128 * u:128 * u + 128] for u in range(4 * h, 4 * h + 4)], 0)
            spread = dot(left, expand[...]).astype(bf16)
            for u in range(4):
                for q in range(2):
                    for p in range(2):
                        lanes = (2 * q + p) * 128
                        grid[r * 32 + 2 * (4 * h + u) + q, 32 * p:32 * p + 32, :] = (
                            spread[32 * u:32 * u + 32, lanes:lanes + 128]
                        )

    for h in range(2):
        for m in (4, 2, 1, 3):
            take(h, m)
    for h in range(2):
        take_sibling(h, 0)
    prepare(row)
    prepare(row + 1 - 2 * core)
    for m in (4, 2, 1, 3):
        prepare(row_peer(m)[0] * 2 + core)
    for m in (5, 7, 6):
        take(0, m)
    for m in (4, 2, 1, 3):
        for h in range(2):
            take_sibling(h, m)
        prepare(row_peer(m)[0] * 2 + 1 - core)
    for m in (5, 7, 6):
        take(1, m)
        prepare(row_peer(m)[0] * 2 + core)
    for m in (5, 7, 6):
        for h in range(2):
            take_sibling(h, m)
        prepare(row_peer(m)[0] * 2 + 1 - core)

    stage_col(0)

    low = lax.broadcasted_iota(jnp.int32, (S, 128), 1) < 64
    group = lax.broadcasted_iota(jnp.int32, (64, 128), 1) // 32

    def block_row(i):
        live = counts[0, i]
        where = []
        for t in range(SLOT):
            g = columns[t, i]
            high = lax.shift_left(lax.shift_right_logical(g, 8), 5)
            where.append(jnp.where(live > t, high + jnp.bitwise_and(g, 31), ZERO_BLOCK))
        v0, v1, v2 = [grid[w] for w in where]
        first = jnp.where(group == 1, v1, jnp.where(group == 2, v2, v0))
        second = jnp.where(group == 0, v1, v2)
        left = jnp.concatenate([first, second], 1)[:, :192]
        res = dot(left, weights[i])
        return res[0:16] + res[16:32], res[32:48] + res[48:64]

    def sum_copy(src, m, dy, dz):
        return pltpu.make_async_remote_copy(
            src, inbox.at[m], s2.at[m], r2.at[m],
            device_id=(row, (yl + dy) % 2 * 4 + (z + dz) % 4), device_id_type=MESH,
        )

    def landed(m):
        sum_copy(inbox.at[m], m, 1, 0).wait_recv()

    def piece(n, proj):
        m = n * 0
        for place, peer in enumerate((6, 5, 7, 1, 3, 2, 4)):
            m = jnp.where(n == place, peer, m)
        d = (yl + m // 4) % 2 * 4 + (z + m % 4) % 4
        for u in range(16):
            even0, odd0 = block_row(d * 32 + 2 * u)
            even1, odd1 = block_row(d * 32 + 2 * u + 1)
            partial[d, :, 128 * u:128 * u + 128] = jnp.where(low, even0, odd1) + pltpu.roll(
                jnp.where(low, even1, odd0), 64, 1
            )

        @pl.when(n == 0)
        def _():
            sum_copy(partial.at[d], 6, 1, 0).start()

        @pl.when((n >= 1) & (n < 5))
        def _():
            sum_copy(partial.at[d], m, 0, m % 4).start()

        @pl.when(n == 5)
        def _():
            landed(6)
            relay[0] = partial[d] + inbox[6]
            sum_copy(relay.at[0], 2, 0, 2).start()

        @pl.when(n == 6)
        def _():
            landed(5)
            landed(7)
            relay[1] = partial[d] + (inbox[5] + inbox[7])
            sum_copy(relay.at[1], 4, 1, 0).start()

        chunk = basis2[:, pl.ds(pl.multiple_of(d * PIECE, PIECE), PIECE)]
        return proj + dot_nt(stacked(partial[d]), chunk)

    proj = lax.fori_loop(0, 8, piece, jnp.zeros((2 * S, 2 * KS), f32))
    both = proj[:, :KS] + proj[:, KS:]
    stage_sib(1, fold(both))
    stage_row(1)
    stage_end(0)
    stage_col(1)

    for m in (1, 3, 2, 4):
        landed(m)
    total = partial[col] + (inbox[1] + inbox[3]) + (inbox[2] + inbox[4])

    def spread(h, k, n, m):
        rows = pl.ds(8 * h, 8)
        send(product.at[k, rows], product.at[k, rows], s3.at[h, n], r3.at[h, k], col_peer(m)[1])

    def spread_wait(h, k):
        rows = pl.ds(8 * h, 8)
        arrival(product.at[k, rows], s3.at[h, 0], r3.at[h, k]).wait_recv()

    product[col] = total
    for m in (4, 2, 1, 3):
        for h in range(2):
            spread(h, col, m, m)

    stage_end(1)
    first_proj = summed(1)
    basis_gram = jnp.concatenate([red_col[0, k] for k in range(8)], 0)
    coeffs = 2.0 * first_proj - jnp.dot(
        first_proj, basis_gram, precision=lax.Precision.HIGHEST, preferred_element_type=f32
    )
    coeffs_out[...] = coeffs
    coeffs2 = wide(coeffs)
    writes = []

    def seen(k):
        chunk = basis2[:, pl.ds(pl.multiple_of(k * PIECE, PIECE), PIECE)]
        return fold(dot(coeffs2, chunk))

    def keep(k, rest):
        rest = stacked(rest)
        twice[k] = rest
        write = pltpu.make_async_copy(twice.at[k], twice_out.at[k], out_sem.at[k])
        write.start()
        writes.append(write)
        return rest

    def remove(m):
        k = col_peer(m)[0]
        if m not in (2, 4):
            for h in range(2):
                spread_wait(h, k)
        keep(k, product[k] - foreseen[k])

    def foresee(*ms):
        for m in ms:
            foreseen[col_peer(m)[0]] = seen(col_peer(m)[0])

    own_rest = keep(col, product[col] - seen(col))
    quads = dot_nt(own_rest, own_rest)
    quads = quads[:, :S] + quads[:, S:]
    stage_sib(2, jnp.concatenate([fold(quads), jnp.zeros((S, 128 - S), f32)], 1))
    for h in range(2):
        k = col_peer(4)[0]
        spread_wait(h, k)
        spread(h, k, 5, 1)
        spread(h, k, 6, 3)
    stage_row(2)
    for h in range(2):
        k = col_peer(2)[0]
        spread_wait(h, k)
        spread(h, k, 7, 4)
    foresee(1, 3, 4, 2)
    stage_col(2)
    foresee(5, 7, 6)
    for m in (1, 3, 4, 2):
        remove(m)
    stage_end(2)

    lane = lax.broadcasted_iota(jnp.int32, (S, 128), 1)
    line = lax.broadcasted_iota(jnp.int32, (S, 128), 0)
    work = jnp.where(lane == line + S, 1.0, summed(2))
    factor = jnp.zeros((S, 128), f32)
    scale = jnp.zeros((S, 128), f32)
    for j in range(S):
        column = jnp.broadcast_to(work[:, j:j + 1], (S, 128))
        pivot = jnp.broadcast_to(column[j:j + 1, :], (S, 128))
        root = lax.rsqrt(pivot)
        factor = jnp.where((lane == j) & (line >= j), column * root, factor)
        scale = jnp.where(line == j, root, scale)
        ratio = jnp.where(line > j, column / pivot, 0.0)
        work = work - ratio * jnp.broadcast_to(work[j:j + 1, :], (S, 128))
    factor_out[...] = factor[:, :S]
    inverse_out[...] = work * scale

    for m in (5, 7, 6):
        remove(m)

    for copy in sends:
        copy.wait_send()
    for m in range(1, 8):
        sum_copy(inbox.at[m], m, 1, 0).wait_send()
    for write in writes:
        write.wait()


def finish(twice_in, coeffs_in, factor_in, inverse_in, out, coeffs_out, factor_out, twice, final, in_sem, out_sem, small_sem):
    loads, writes = [], []
    for k in range(8):
        loads.append(pltpu.make_async_copy(twice_in.at[k], twice.at[k], in_sem.at[k]))
    writes.append(pltpu.make_async_copy(coeffs_in, coeffs_out, small_sem.at[0]))
    writes.append(pltpu.make_async_copy(factor_in, factor_out, small_sem.at[1]))
    for copy in loads + writes:
        copy.start()
    inverse2 = wide(inverse_in[...][:, S:2 * S])
    for k in range(8):
        loads[k].wait()
        final[k] = fold(dot(inverse2, twice[k]))
        write = pltpu.make_async_copy(final.at[k], out.at[:, pl.ds(k * PIECE, PIECE)], out_sem.at[k])
        write.start()
        writes.append(write)
    for write in writes:
        write.wait()


def body(blocks, columns, counts, old_basis, vectors):
    bands = blocks.reshape(ROWS // BAND, BAND, SLOT, 32, 128).transpose(2, 0, 3, 1, 4)
    bands = bands.reshape(SLOT, ROWS // BAND, 32 * BAND, 128)
    D = pltpu.SemaphoreType.DMA
    V = pltpu.VMEM
    any_space = pl.BlockSpec(memory_space=pl.ANY)
    smem = pl.BlockSpec(memory_space=pltpu.SMEM)
    vmem = pl.BlockSpec(memory_space=pltpu.VMEM)
    twice, coeffs, factor, inverse = pl.pallas_call(
        kernel,
        out_shape=(
            jax.ShapeDtypeStruct((8, 2 * S, PIECE), bf16),
            jax.ShapeDtypeStruct((S, KS), f32),
            jax.ShapeDtypeStruct((S, S), f32),
            jax.ShapeDtypeStruct((S, 128), f32),
        ),
        in_specs=[smem, smem, any_space, any_space, any_space],
        out_specs=(any_space, vmem, vmem, vmem),
        scratch_shapes=[
            V((SLOT, ROWS // BAND, 32 * BAND, 128), f32),
            V((ROWS, 192, 128), bf16),
            V((ZERO_BLOCK + 1, 64, 128), bf16),
            V((128, 512), bf16),
            V((2, KS, PIECE), f32),
            V((2 * KS, UNK), bf16),
            V((2, 16, S // 2, PIECE), f32),
            V((8, S, PIECE), f32),
            V((8, S, PIECE), f32),
            V((2, S, PIECE), f32),
            V((8, S, PIECE), f32),
            V((8, S, PIECE), f32),
            V((8, 2 * S, PIECE), bf16),
            V((3, 1, S, 128), f32),
            V((3, S, 128), f32),
            V((3, 8, S, 128), f32),
            V((3, 8, S, 128), f32),
            D((SLOT,)), D((2,)), D((2,)), D((8,)),
            D((2, 18)), D((2, 16)), D((8,)), D((8,)), D((2, 8)), D((2, 8)),
            D((3,)), D((3,)), D((3, 8)), D((3, 8)), D((3, 8)), D((3, 8)),
        ],
        compiler_params=pltpu.CompilerParams(
            collective_id=0, has_side_effects=True, vmem_limit_bytes=62 << 20
        ),
    )(columns.T, counts.T, bands, vectors, old_basis)
    new_block, coeffs, factor = pl.pallas_call(
        finish,
        out_shape=(
            jax.ShapeDtypeStruct((S, UNK), f32),
            jax.ShapeDtypeStruct((S, KS), f32),
            jax.ShapeDtypeStruct((S, S), f32),
        ),
        in_specs=[any_space, any_space, any_space, vmem],
        out_specs=(any_space, any_space, any_space),
        scratch_shapes=[V((8, 2 * S, PIECE), bf16), V((8, S, PIECE), f32), D((8,)), D((8,)), D((2,))],
        compiler_params=pltpu.CompilerParams(vmem_limit_bytes=62 << 20),
    )(twice, coeffs, factor, inverse)
    return new_block, coeffs.T, factor


def solution(mesh):
    return jax.shard_map(
        body,
        mesh=mesh,
        in_specs=(
            P("row", "col", None),
            P("row", "col"),
            P("row", "col"),
            P(None, "row"),
            P(None, "row"),
        ),
        out_specs=(P(None, "row"), P(), P()),
        check_vma=False,
    )
```

```python
import functools

import jax
import jax.numpy as jnp
from jax import lax
from jax.experimental import pallas as pl
from jax.experimental.pallas import tpu as pltpu
from jax.sharding import PartitionSpec as P

f32 = jnp.float32
bf16 = jnp.bfloat16
MESH = pl.DeviceIdType.MESH

B = 64
S = 16
SLOT = 3
BAND = 8
ROWS = 256
PIECE = 2048
UNK = 16384
KS = 128
TOTAL = 262144
ZERO_BLOCK = 512


def split(x):
    hi = x.astype(bf16)
    return hi, (x - hi.astype(f32)).astype(bf16)


def stacked(x):
    hi, lo = split(x)
    return jnp.concatenate([hi, lo], 0)


def fold(x):
    return x[:S] + x[S:]


def wide(x):
    two = stacked(x)
    return jnp.concatenate([two, two], 1)


def dot(a, b):
    return jnp.dot(a, b, preferred_element_type=f32)


def dot_nt(a, b):
    return lax.dot_general(a, b, (((1,), (1,)), ((), ())), preferred_element_type=f32)


def exact(a, b):
    return jnp.dot(a, b, precision=lax.Precision.HIGHEST, preferred_element_type=f32)


def exact_nt(a, b):
    return lax.dot_general(
        a, b, (((1,), (1,)), ((), ())), precision=lax.Precision.HIGHEST, preferred_element_type=f32
    )


def kernel(
    columns, counts, blocks, vectors, basis,
    twice_out, coeffs_out, factor_out, inverse_out,
    stage, weights, grid, expand, basis_stage, basis2, pieces, partial, inbox, relay, foreseen, product, twice,
    red_src, red_sib, red_row, red_col,
    load_sem, basis_sem, own_sem, out_sem,
    s1, r1, s2, r2, s3, r3, sib_s, sib_r, row_s, row_r, col_s, col_r,
):
    row = lax.axis_index("row")
    col = lax.axis_index("col")
    yh, x, core = row // 8, row // 2 % 4, row % 2
    yl, z = col // 4, col % 4
    chip = yh * 4 + x
    sibling = (row + 1 - 2 * core, col)

    def row_peer(m):
        c = (yh + m // 4) % 2 * 4 + (x + m % 4) % 4
        return c, (c * 2 + core, col)

    def col_peer(m):
        k = (yl + m // 4) % 2 * 4 + (z + m % 4) % 4
        return k, (row, k)

    own_loads = []
    for h in range(2):
        own_loads.append(
            pltpu.make_async_copy(
                vectors.at[8 * h:8 * h + 8, pl.ds(pl.multiple_of(col * PIECE, PIECE), PIECE)],
                pieces.at[h, row],
                own_sem.at[h],
            )
        )
        own_loads[h].start()
    loads = []
    for s in range(SLOT):
        load = pltpu.make_async_copy(blocks.at[s], stage.at[s], load_sem.at[s])
        load.start()
        loads.append(load)

    def basis_load(c):
        return pltpu.make_async_copy(
            basis.at[:, pl.ds(c * PIECE, PIECE)], basis_stage.at[c % 2], basis_sem.at[c % 2]
        )

    basis_load(0).start()
    basis_load(1).start()

    barrier = pltpu.get_barrier_semaphore()
    peers = [sibling] + [row_peer(m)[1] for m in range(1, 8)] + [col_peer(m)[1] for m in range(1, 8)]
    for peer in peers:
        pl.semaphore_signal(barrier, inc=1, device_id=peer, device_id_type=MESH)

    cell = lax.broadcasted_iota(jnp.int32, (128, 512), 0)
    spot = lax.broadcasted_iota(jnp.int32, (128, 512), 1)
    expand[...] = jnp.where(
        cell == spot // 256 * 64 + spot % 32 * 2 + spot // 128 % 2, 1.0, 0.0
    ).astype(bf16)
    grid[ZERO_BLOCK] = jnp.zeros((64, 128), bf16)

    for s in range(SLOT):
        loads[s].wait()

        @pl.loop(0, ROWS // BAND)
        def _(band, s=s):
            for i in range(BAND):
                hi, lo = split(stage[s, band, pl.ds(i, 32, stride=BAND), :])
                weights[band * BAND + i, 32 * s:32 * s + 32, :] = hi
                weights[band * BAND + i, 96 + 32 * s:128 + 32 * s, :] = lo

    pl.semaphore_wait(barrier, len(peers))

    sends = []

    def send(src, dst, ssem, rsem, peer):
        copy = pltpu.make_async_remote_copy(src, dst, ssem, rsem, device_id=peer, device_id_type=MESH)
        copy.start()
        sends.append(copy)

    def arrival(dst, ssem, rsem):
        return pltpu.make_async_remote_copy(dst, dst, ssem, rsem, device_id=sibling, device_id_type=MESH)

    def pass_on(h, r, n, peer):
        send(pieces.at[h, r], pieces.at[h, r], s1.at[h, n], r1.at[h, r], peer)

    for h in range(2):
        own_loads[h].wait()
        for m in (4, 2):
            pass_on(h, row, m, row_peer(m)[1])
    for h in range(2):
        for m in (1, 3):
            pass_on(h, row, m, row_peer(m)[1])
        pass_on(h, row, 0, sibling)

    def take(h, m):
        r = row_peer(m)[0] * 2 + core
        arrival(pieces.at[h, r], s1.at[h, 0], r1.at[h, r]).wait_recv()
        if m == 4:
            pass_on(h, r, 8, row_peer(1)[1])
            pass_on(h, r, 9, row_peer(3)[1])
        if m == 2:
            pass_on(h, r, 10, row_peer(4)[1])
        pass_on(h, r, 10 + m, sibling)

    def take_sibling(h, m):
        r = row_peer(m)[0] * 2 + 1 - core
        arrival(pieces.at[h, r], s1.at[h, 0], r1.at[h, r]).wait_recv()

    own_basis = pl.multiple_of(col * 16, 16)
    gram_rows = jnp.zeros((2 * S, 2 * KS), f32)
    for c in range(8):
        basis_load(c).wait()
        chunk = stacked(basis_stage[c % 2])
        basis2[:, c * PIECE:(c + 1) * PIECE] = chunk
        if c + 2 < 8:
            basis_load(c + 2).start()
        left = jnp.concatenate(
            [
                basis2[pl.ds(own_basis, 16), c * PIECE:(c + 1) * PIECE],
                basis2[pl.ds(KS + own_basis, 16), c * PIECE:(c + 1) * PIECE],
            ],
            0,
        )
        gram_rows += dot_nt(left, chunk)

    def stage_sib(n, value):
        red_src[n, 0] = value
        send(red_src.at[n, 0], red_sib.at[n], sib_s.at[n], sib_r.at[n], sibling)

    def stage_row(n):
        arrival(red_sib.at[n], sib_s.at[n], sib_r.at[n]).wait_recv()
        red_row[n, chip] = red_src[n, 0] + red_sib[n]
        for m in range(1, 8):
            send(red_row.at[n, chip], red_row.at[n, chip], row_s.at[n, m], row_r.at[n, chip], row_peer(m)[1])

    def stage_col(n):
        for m in range(1, 8):
            c = row_peer(m)[0]
            arrival(red_row.at[n, c], row_s.at[n, m], row_r.at[n, c]).wait_recv()
        total = red_row[n, 0]
        for c in range(1, 8):
            total += red_row[n, c]
        red_col[n, col] = total * (1.0 / TOTAL)
        for m in range(1, 8):
            send(red_col.at[n, col], red_col.at[n, col], col_s.at[n, m], col_r.at[n, col], col_peer(m)[1])

    def stage_end(n):
        for m in range(1, 8):
            k = col_peer(m)[0]
            arrival(red_col.at[n, k], col_s.at[n, m], col_r.at[n, k]).wait_recv()

    def summed(n):
        total = red_col[n, 0]
        for k in range(1, 8):
            total += red_col[n, k]
        return total

    both = gram_rows[:, :KS] + gram_rows[:, KS:]
    stage_sib(0, fold(both))
    stage_row(0)

    def prepare(r):
        two = stacked(jnp.concatenate([pieces[0, r], pieces[1, r]], 0))
        for h in range(4):
            left = jnp.concatenate([two[:, 128 * u:128 * u + 128] for u in range(4 * h, 4 * h + 4)], 0)
            spread = dot(left, expand[...]).astype(bf16)
            for u in range(4):
                for q in range(2):
                    for p in range(2):
                        lanes = (2 * q + p) * 128
                        grid[r * 32 + 2 * (4 * h + u) + q, 32 * p:32 * p + 32, :] = (
                            spread[32 * u:32 * u + 32, lanes:lanes + 128]
                        )

    for h in range(2):
        for m in (4, 2, 1, 3):
            take(h, m)
    for h in range(2):
        take_sibling(h, 0)
    prepare(row)
    prepare(row + 1 - 2 * core)
    for m in (4, 2, 1, 3):
        prepare(row_peer(m)[0] * 2 + core)
    for m in (5, 7, 6):
        take(0, m)
    for m in (4, 2, 1, 3):
        for h in range(2):
            take_sibling(h, m)
        prepare(row_peer(m)[0] * 2 + 1 - core)
    for m in (5, 7, 6):
        take(1, m)
        prepare(row_peer(m)[0] * 2 + core)
    for m in (5, 7, 6):
        for h in range(2):
            take_sibling(h, m)
        prepare(row_peer(m)[0] * 2 + 1 - core)

    stage_col(0)

    low = lax.broadcasted_iota(jnp.int32, (S, 128), 1) < 64
    group = lax.broadcasted_iota(jnp.int32, (64, 128), 1) // 32

    def block_row(i):
        live = counts[0, i]
        where = []
        for t in range(SLOT):
            g = columns[t, i]
            high = lax.shift_left(lax.shift_right_logical(g, 8), 5)
            where.append(jnp.where(live > t, high + jnp.bitwise_and(g, 31), ZERO_BLOCK))
        v0, v1, v2 = [grid[w] for w in where]
        first = jnp.where(group == 1, v1, jnp.where(group == 2, v2, v0))
        second = jnp.where(group == 0, v1, v2)
        left = jnp.concatenate([first, second], 1)[:, :192]
        res = dot(left, weights[i])
        return res[0:16] + res[16:32], res[32:48] + res[48:64]

    def sum_copy(src, m, dy, dz):
        return pltpu.make_async_remote_copy(
            src, inbox.at[m], s2.at[m], r2.at[m],
            device_id=(row, (yl + dy) % 2 * 4 + (z + dz) % 4), device_id_type=MESH,
        )

    def landed(m):
        sum_copy(inbox.at[m], m, 1, 0).wait_recv()

    def turn(n):
        m = n * 0
        for place, peer in enumerate((6, 5, 7, 1, 3, 2, 4)):
            m = jnp.where(n == place, peer, m)
        return m, (yl + m // 4) % 2 * 4 + (z + m % 4) % 4

    @pl.loop(0, 8)
    def _(n):
        m, d = turn(n)
        for u in range(16):
            even0, odd0 = block_row(d * 32 + 2 * u)
            even1, odd1 = block_row(d * 32 + 2 * u + 1)
            partial[d, :, 128 * u:128 * u + 128] = jnp.where(low, even0, odd1) + pltpu.roll(
                jnp.where(low, even1, odd0), 64, 1
            )

        @pl.when(n == 0)
        def _():
            sum_copy(partial.at[d], 6, 1, 0).start()

        @pl.when((n >= 1) & (n < 5))
        def _():
            sum_copy(partial.at[d], m, 0, m % 4).start()

    def project(n, proj):
        d = turn(n)[1]
        chunk = basis2[:, pl.ds(pl.multiple_of(d * PIECE, PIECE), PIECE)]
        return proj + dot_nt(stacked(partial[d]), chunk)

    proj = lax.fori_loop(0, 3, project, jnp.zeros((2 * S, 2 * KS), f32))
    landed(6)
    relay[0] = partial[col_peer(2)[0]] + inbox[6]
    sum_copy(relay.at[0], 2, 0, 2).start()
    proj = lax.fori_loop(3, 8, project, proj)
    landed(5)
    landed(7)
    relay[1] = partial[col_peer(4)[0]] + (inbox[5] + inbox[7])
    sum_copy(relay.at[1], 4, 1, 0).start()
    both = proj[:, :KS] + proj[:, KS:]
    stage_sib(1, fold(both))
    stage_row(1)
    for m in (1, 3, 2, 4):
        landed(m)
    total = partial[col] + (inbox[1] + inbox[3]) + (inbox[2] + inbox[4])

    def spread(h, k, n, m):
        rows = pl.ds(8 * h, 8)
        send(product.at[k, rows], product.at[k, rows], s3.at[h, n], r3.at[h, k], col_peer(m)[1])

    def spread_wait(h, k):
        rows = pl.ds(8 * h, 8)
        arrival(product.at[k, rows], s3.at[h, 0], r3.at[h, k]).wait_recv()

    product[col] = total
    own_product = stacked(total)
    quads = dot_nt(own_product, own_product)
    quads = quads[:, :S] + quads[:, S:]
    stage_sib(2, jnp.concatenate([fold(quads), jnp.zeros((S, 128 - S), f32)], 1))
    for m in (2, 1, 3):
        for h in range(2):
            spread(h, col, m, m)
    stage_end(0)
    stage_col(1)
    stage_row(2)
    for h in range(2):
        spread(h, col, 4, 4)
    stage_col(2)

    stage_end(1)
    first_proj = summed(1)
    basis_gram = jnp.concatenate([red_col[0, k] for k in range(8)], 0)
    coeffs = 2.0 * first_proj - exact(first_proj, basis_gram)
    left_over = first_proj - exact(coeffs, basis_gram)
    removed = exact_nt(
        jnp.concatenate([first_proj, coeffs], 1), jnp.concatenate([coeffs, left_over], 1)
    )
    coeffs_out[...] = coeffs
    coeffs2 = wide(coeffs)
    writes = []

    def seen(k):
        chunk = basis2[:, pl.ds(pl.multiple_of(k * PIECE, PIECE), PIECE)]
        return fold(dot(coeffs2, chunk))

    def keep(k, rest):
        rest = stacked(rest)
        twice[k] = rest
        write = pltpu.make_async_copy(twice.at[k], twice_out.at[k], out_sem.at[k])
        write.start()
        writes.append(write)
        return rest

    def remove(m):
        k = col_peer(m)[0]
        if m not in (2, 4):
            for h in range(2):
                spread_wait(h, k)
        keep(k, product[k] - foreseen[k])

    def foresee(*ms):
        for m in ms:
            foreseen[col_peer(m)[0]] = seen(col_peer(m)[0])

    def hand_on(m, *next_peers):
        k = col_peer(m)[0]
        for h in range(2):
            spread_wait(h, k)
            for n, peer in next_peers:
                spread(h, k, n, peer)

    hand_on(4, (5, 1), (6, 3))
    hand_on(2, (7, 4))
    keep(col, product[col] - seen(col))
    foresee(1, 3, 4, 2, 5, 7, 6)
    for m in (1, 3, 4, 2):
        remove(m)
    stage_end(2)

    lane = lax.broadcasted_iota(jnp.int32, (S, 128), 1)
    line = lax.broadcasted_iota(jnp.int32, (S, 128), 0)
    gram = summed(2) - jnp.concatenate([removed, jnp.zeros((S, 128 - S), f32)], 1)
    work = jnp.where(lane == line + S, 1.0, gram)
    factor = jnp.zeros((S, 128), f32)
    scale = jnp.zeros((S, 128), f32)
    for j in range(S):
        column = jnp.broadcast_to(work[:, j:j + 1], (S, 128))
        pivot = jnp.broadcast_to(column[j:j + 1, :], (S, 128))
        root = lax.rsqrt(pivot)
        factor = jnp.where((lane == j) & (line >= j), column * root, factor)
        scale = jnp.where(line == j, root, scale)
        ratio = jnp.where(line > j, column / pivot, 0.0)
        work = work - ratio * jnp.broadcast_to(work[j:j + 1, :], (S, 128))
    factor_out[...] = factor[:, :S]
    inverse_out[...] = work * scale

    for m in (5, 7, 6):
        remove(m)

    for copy in sends:
        copy.wait_send()
    for m in range(1, 8):
        sum_copy(inbox.at[m], m, 1, 0).wait_send()
    for write in writes:
        write.wait()


def finish(twice_in, coeffs_in, factor_in, inverse_in, out, coeffs_out, factor_out, twice, final, in_sem, out_sem, small_sem):
    loads, writes = [], []
    for k in range(8):
        loads.append(pltpu.make_async_copy(twice_in.at[k], twice.at[k], in_sem.at[k]))
    writes.append(pltpu.make_async_copy(coeffs_in, coeffs_out, small_sem.at[0]))
    writes.append(pltpu.make_async_copy(factor_in, factor_out, small_sem.at[1]))
    for copy in loads + writes:
        copy.start()
    inverse2 = wide(inverse_in[...][:, S:2 * S])
    for k in range(8):
        loads[k].wait()
        final[k] = fold(dot(inverse2, twice[k]))
        write = pltpu.make_async_copy(final.at[k], out.at[:, pl.ds(k * PIECE, PIECE)], out_sem.at[k])
        write.start()
        writes.append(write)
    for write in writes:
        write.wait()


def body(blocks, columns, counts, old_basis, vectors):
    bands = blocks.reshape(ROWS // BAND, BAND, SLOT, 32, 128).transpose(2, 0, 3, 1, 4)
    bands = bands.reshape(SLOT, ROWS // BAND, 32 * BAND, 128)
    D = pltpu.SemaphoreType.DMA
    V = pltpu.VMEM
    any_space = pl.BlockSpec(memory_space=pl.ANY)
    smem = pl.BlockSpec(memory_space=pltpu.SMEM)
    vmem = pl.BlockSpec(memory_space=pltpu.VMEM)
    twice, coeffs, factor, inverse = pl.pallas_call(
        kernel,
        out_shape=(
            jax.ShapeDtypeStruct((8, 2 * S, PIECE), bf16),
            jax.ShapeDtypeStruct((S, KS), f32),
            jax.ShapeDtypeStruct((S, S), f32),
            jax.ShapeDtypeStruct((S, 128), f32),
        ),
        in_specs=[smem, smem, any_space, any_space, any_space],
        out_specs=(any_space, vmem, vmem, vmem),
        scratch_shapes=[
            V((SLOT, ROWS // BAND, 32 * BAND, 128), f32),
            V((ROWS, 192, 128), bf16),
            V((ZERO_BLOCK + 1, 64, 128), bf16),
            V((128, 512), bf16),
            V((2, KS, PIECE), f32),
            V((2 * KS, UNK), bf16),
            V((2, 16, S // 2, PIECE), f32),
            V((8, S, PIECE), f32),
            V((8, S, PIECE), f32),
            V((2, S, PIECE), f32),
            V((8, S, PIECE), f32),
            V((8, S, PIECE), f32),
            V((8, 2 * S, PIECE), bf16),
            V((3, 1, S, 128), f32),
            V((3, S, 128), f32),
            V((3, 8, S, 128), f32),
            V((3, 8, S, 128), f32),
            D((SLOT,)), D((2,)), D((2,)), D((8,)),
            D((2, 18)), D((2, 16)), D((8,)), D((8,)), D((2, 8)), D((2, 8)),
            D((3,)), D((3,)), D((3, 8)), D((3, 8)), D((3, 8)), D((3, 8)),
        ],
        compiler_params=pltpu.CompilerParams(
            collective_id=0, has_side_effects=True, vmem_limit_bytes=62 << 20
        ),
    )(columns.T, counts.T, bands, vectors, old_basis)
    new_block, coeffs, factor = pl.pallas_call(
        finish,
        out_shape=(
            jax.ShapeDtypeStruct((S, UNK), f32),
            jax.ShapeDtypeStruct((S, KS), f32),
            jax.ShapeDtypeStruct((S, S), f32),
        ),
        in_specs=[any_space, any_space, any_space, vmem],
        out_specs=(any_space, any_space, any_space),
        scratch_shapes=[V((8, 2 * S, PIECE), bf16), V((8, S, PIECE), f32), D((8,)), D((8,)), D((2,))],
        compiler_params=pltpu.CompilerParams(vmem_limit_bytes=62 << 20),
    )(twice, coeffs, factor, inverse)
    return new_block, coeffs.T, factor


def solution(mesh):
    return jax.shard_map(
        body,
        mesh=mesh,
        in_specs=(
            P("row", "col", None),
            P("row", "col"),
            P("row", "col"),
            P(None, "row"),
            P(None, "row"),
        ),
        out_specs=(P(None, "row"), P(), P()),
        check_vma=False,
    )
```

```python
import functools

import jax
import jax.numpy as jnp
from jax import lax
from jax.experimental import pallas as pl
from jax.experimental.pallas import tpu as pltpu
from jax.sharding import PartitionSpec as P

f32 = jnp.float32
bf16 = jnp.bfloat16
MESH = pl.DeviceIdType.MESH

B = 64
S = 16
SLOT = 3
BAND = 8
ROWS = 256
PIECE = 2048
UNK = 16384
KS = 128
TOTAL = 262144
ZERO_BLOCK = 512


def split(x):
    hi = x.astype(bf16)
    return hi, (x - hi.astype(f32)).astype(bf16)


def stacked(x):
    hi, lo = split(x)
    return jnp.concatenate([hi, lo], 0)


def fold(x):
    return x[:S] + x[S:]


def wide(x):
    two = stacked(x)
    return jnp.concatenate([two, two], 1)


def dot(a, b):
    return jnp.dot(a, b, preferred_element_type=f32)


def dot_nt(a, b):
    return lax.dot_general(a, b, (((1,), (1,)), ((), ())), preferred_element_type=f32)


def exact(a, b):
    return jnp.dot(a, b, precision=lax.Precision.HIGHEST, preferred_element_type=f32)


def exact_nt(a, b):
    return lax.dot_general(
        a, b, (((1,), (1,)), ((), ())), precision=lax.Precision.HIGHEST, preferred_element_type=f32
    )


def kernel(
    columns_in, counts_in, blocks, vectors, basis,
    twice_out, coeffs_out, factor_out, inverse_out,
    columns, counts, small, stage, weights, grid, expand, basis_stage, basis2, pieces, partial, inbox, relay, foreseen, product, twice,
    red_src, red_sib, red_row, red_col,
    index_sem, small_sem, load_sem, basis_sem, own_sem, out_sem,
    s1, r1, s2, r2, s3, r3, sib_s, sib_r, row_s, row_r, col_s, col_r,
):
    row = lax.axis_index("row")
    col = lax.axis_index("col")
    yh, x, core = row // 8, row // 2 % 4, row % 2
    yl, z = col // 4, col % 4
    chip = yh * 4 + x
    sibling = (row + 1 - 2 * core, col)

    def row_peer(m):
        c = (yh + m // 4) % 2 * 4 + (x + m % 4) % 4
        return c, (c * 2 + core, col)

    def col_peer(m):
        k = (yl + m // 4) % 2 * 4 + (z + m % 4) % 4
        return k, (row, k)

    barrier = pltpu.get_barrier_semaphore()
    peers = [sibling] + [row_peer(m)[1] for m in range(1, 8)] + [col_peer(m)[1] for m in range(1, 8)]
    for peer in peers:
        pl.semaphore_signal(barrier, inc=1, device_id=peer, device_id_type=MESH)

    index_loads = [
        pltpu.make_async_copy(columns_in, columns, index_sem.at[0]),
        pltpu.make_async_copy(counts_in, counts, index_sem.at[1]),
    ]
    for load in index_loads:
        load.start()
    own_loads = []
    for h in range(2):
        own_loads.append(
            pltpu.make_async_copy(
                vectors.at[8 * h:8 * h + 8, pl.ds(pl.multiple_of(col * PIECE, PIECE), PIECE)],
                pieces.at[h, row],
                own_sem.at[h],
            )
        )
        own_loads[h].start()
    loads = []
    for s in range(SLOT):
        load = pltpu.make_async_copy(blocks.at[s], stage.at[s], load_sem.at[s])
        load.start()
        loads.append(load)

    def basis_load(c):
        return pltpu.make_async_copy(
            basis.at[:, pl.ds(c * PIECE, PIECE)], basis_stage.at[c % 2], basis_sem.at[c % 2]
        )

    basis_load(0).start()
    basis_load(1).start()

    cell = lax.broadcasted_iota(jnp.int32, (128, 512), 0)
    spot = lax.broadcasted_iota(jnp.int32, (128, 512), 1)
    expand[...] = jnp.where(
        cell == spot // 256 * 64 + spot % 32 * 2 + spot // 128 % 2, 1.0, 0.0
    ).astype(bf16)
    grid[ZERO_BLOCK] = jnp.zeros((64, 128), bf16)

    for s in range(SLOT):
        loads[s].wait()

        @pl.loop(0, ROWS // BAND)
        def _(band, s=s):
            for i in range(BAND):
                hi, lo = split(stage[s, band, pl.ds(i, 32, stride=BAND), :])
                weights[band * BAND + i, 32 * s:32 * s + 32, :] = hi
                weights[band * BAND + i, 96 + 32 * s:128 + 32 * s, :] = lo

    pl.semaphore_wait(barrier, len(peers))
    for load in index_loads:
        load.wait()

    sends = []

    def send(src, dst, ssem, rsem, peer):
        copy = pltpu.make_async_remote_copy(src, dst, ssem, rsem, device_id=peer, device_id_type=MESH)
        copy.start()
        sends.append(copy)

    def arrival(dst, ssem, rsem):
        return pltpu.make_async_remote_copy(dst, dst, ssem, rsem, device_id=sibling, device_id_type=MESH)

    def pass_on(h, r, n, peer):
        send(pieces.at[h, r], pieces.at[h, r], s1.at[h, n], r1.at[h, r], peer)

    for h in range(2):
        own_loads[h].wait()
        for m in (4, 2):
            pass_on(h, row, m, row_peer(m)[1])
    for h in range(2):
        for m in (1, 3):
            pass_on(h, row, m, row_peer(m)[1])
        pass_on(h, row, 0, sibling)

    def take(h, m):
        r = row_peer(m)[0] * 2 + core
        arrival(pieces.at[h, r], s1.at[h, 0], r1.at[h, r]).wait_recv()
        if m == 4:
            pass_on(h, r, 8, row_peer(1)[1])
            pass_on(h, r, 9, row_peer(3)[1])
        if m == 2:
            pass_on(h, r, 10, row_peer(4)[1])
        pass_on(h, r, 10 + m, sibling)

    def take_sibling(h, m):
        r = row_peer(m)[0] * 2 + 1 - core
        arrival(pieces.at[h, r], s1.at[h, 0], r1.at[h, r]).wait_recv()

    own_basis = pl.multiple_of(col * 16, 16)
    gram_rows = jnp.zeros((2 * S, 2 * KS), f32)
    for c in range(8):
        basis_load(c).wait()
        chunk = stacked(basis_stage[c % 2])
        basis2[:, c * PIECE:(c + 1) * PIECE] = chunk
        if c + 2 < 8:
            basis_load(c + 2).start()
        left = jnp.concatenate(
            [
                basis2[pl.ds(own_basis, 16), c * PIECE:(c + 1) * PIECE],
                basis2[pl.ds(KS + own_basis, 16), c * PIECE:(c + 1) * PIECE],
            ],
            0,
        )
        gram_rows += dot_nt(left, chunk)

    def stage_sib(n, value):
        red_src[n, 0] = value
        send(red_src.at[n, 0], red_sib.at[n], sib_s.at[n], sib_r.at[n], sibling)

    def stage_row(n):
        arrival(red_sib.at[n], sib_s.at[n], sib_r.at[n]).wait_recv()
        red_row[n, chip] = red_src[n, 0] + red_sib[n]
        for m in range(1, 8):
            send(red_row.at[n, chip], red_row.at[n, chip], row_s.at[n, m], row_r.at[n, chip], row_peer(m)[1])

    def stage_col(n):
        for m in range(1, 8):
            c = row_peer(m)[0]
            arrival(red_row.at[n, c], row_s.at[n, m], row_r.at[n, c]).wait_recv()
        total = red_row[n, 0]
        for c in range(1, 8):
            total += red_row[n, c]
        red_col[n, col] = total * (1.0 / TOTAL)
        for m in range(1, 8):
            send(red_col.at[n, col], red_col.at[n, col], col_s.at[n, m], col_r.at[n, col], col_peer(m)[1])

    def stage_end(n):
        for m in range(1, 8):
            k = col_peer(m)[0]
            arrival(red_col.at[n, k], col_s.at[n, m], col_r.at[n, k]).wait_recv()

    def summed(n):
        total = red_col[n, 0]
        for k in range(1, 8):
            total += red_col[n, k]
        return total

    both = gram_rows[:, :KS] + gram_rows[:, KS:]
    stage_sib(0, fold(both))
    stage_row(0)

    def prepare(r):
        two = stacked(jnp.concatenate([pieces[0, r], pieces[1, r]], 0))
        for h in range(4):
            left = jnp.concatenate([two[:, 128 * u:128 * u + 128] for u in range(4 * h, 4 * h + 4)], 0)
            spread = dot(left, expand[...]).astype(bf16)
            for u in range(4):
                for q in range(2):
                    for p in range(2):
                        lanes = (2 * q + p) * 128
                        grid[r * 32 + 2 * (4 * h + u) + q, 32 * p:32 * p + 32, :] = (
                            spread[32 * u:32 * u + 32, lanes:lanes + 128]
                        )

    for h in range(2):
        for m in (4, 2, 1, 3):
            take(h, m)
    prepare(row)
    for h in range(2):
        take_sibling(h, 0)
    prepare(row + 1 - 2 * core)
    for m in (4, 2, 1, 3):
        prepare(row_peer(m)[0] * 2 + core)
        for h in range(2):
            take_sibling(h, m)
        prepare(row_peer(m)[0] * 2 + 1 - core)
    for h in range(2):
        for m in (5, 7, 6):
            take(h, m)
    for m in (5, 7, 6):
        prepare(row_peer(m)[0] * 2 + core)
        for h in range(2):
            take_sibling(h, m)
        prepare(row_peer(m)[0] * 2 + 1 - core)

    stage_col(0)

    low = lax.broadcasted_iota(jnp.int32, (S, 128), 1) < 64
    group = lax.broadcasted_iota(jnp.int32, (64, 128), 1) // 32

    def block_row(i):
        live = counts[0, i]
        where = []
        for t in range(SLOT):
            g = columns[t, i]
            high = lax.shift_left(lax.shift_right_logical(g, 8), 5)
            where.append(jnp.where(live > t, high + jnp.bitwise_and(g, 31), ZERO_BLOCK))
        v0, v1, v2 = [grid[w] for w in where]
        first = jnp.where(group == 1, v1, jnp.where(group == 2, v2, v0))
        second = jnp.where(group == 0, v1, v2)
        left = jnp.concatenate([first, second], 1)[:, :192]
        res = dot(left, weights[i])
        return res[0:16] + res[16:32], res[32:48] + res[48:64]

    def sum_copy(src, m, dy, dz):
        return pltpu.make_async_remote_copy(
            src, inbox.at[m], s2.at[m], r2.at[m],
            device_id=(row, (yl + dy) % 2 * 4 + (z + dz) % 4), device_id_type=MESH,
        )

    def landed(m):
        sum_copy(inbox.at[m], m, 1, 0).wait_recv()

    def turn(n):
        m = n * 0
        for place, peer in enumerate((5, 7, 6, 1, 3, 2, 4)):
            m = jnp.where(n == place, peer, m)
        return m, (yl + m // 4) % 2 * 4 + (z + m % 4) % 4

    @pl.loop(0, 8)
    def _(n):
        m, d = turn(n)
        for u in range(16):
            even0, odd0 = block_row(d * 32 + 2 * u)
            even1, odd1 = block_row(d * 32 + 2 * u + 1)
            partial[d, :, 128 * u:128 * u + 128] = jnp.where(low, even0, odd1) + pltpu.roll(
                jnp.where(low, even1, odd0), 64, 1
            )

        @pl.when(n == 2)
        def _():
            sum_copy(partial.at[d], 6, 1, 0).start()

        @pl.when((n < 5) & (n != 2))
        def _():
            sum_copy(partial.at[d], m, 0, m % 4).start()

    def project(n, proj):
        d = turn(n)[1]
        chunk = basis2[:, pl.ds(pl.multiple_of(d * PIECE, PIECE), PIECE)]
        return proj + dot_nt(stacked(partial[d]), chunk)

    proj = lax.fori_loop(0, 4, project, jnp.zeros((2 * S, 2 * KS), f32))
    landed(5)
    landed(7)
    relay[1] = partial[col_peer(4)[0]] + (inbox[5] + inbox[7])
    sum_copy(relay.at[1], 4, 1, 0).start()
    proj = lax.fori_loop(4, 6, project, proj)
    landed(6)
    relay[0] = partial[col_peer(2)[0]] + inbox[6]
    sum_copy(relay.at[0], 2, 0, 2).start()
    proj = lax.fori_loop(6, 8, project, proj)
    both = proj[:, :KS] + proj[:, KS:]
    stage_sib(1, fold(both))
    stage_row(1)
    for m in (1, 3, 2, 4):
        landed(m)
    total = partial[col] + (inbox[1] + inbox[3]) + (inbox[2] + inbox[4])

    def spread(h, k, n, m):
        rows = pl.ds(8 * h, 8)
        send(product.at[k, rows], product.at[k, rows], s3.at[h, n], r3.at[h, k], col_peer(m)[1])

    def spread_wait(h, k):
        rows = pl.ds(8 * h, 8)
        arrival(product.at[k, rows], s3.at[h, 0], r3.at[h, k]).wait_recv()

    product[col] = total
    for m in (4, 2, 1, 3):
        for h in range(2):
            spread(h, col, m, m)
    stage_end(0)
    stage_col(1)
    own_product = stacked(total)
    quads = dot_nt(own_product, own_product)
    quads = quads[:, :S] + quads[:, S:]
    stage_sib(2, jnp.concatenate([fold(quads), jnp.zeros((S, 128 - S), f32)], 1))
    stage_row(2)

    def hand_on(m, *next_peers):
        k = col_peer(m)[0]
        for h in range(2):
            spread_wait(h, k)
            for n, peer in next_peers:
                spread(h, k, n, peer)

    hand_on(4, (5, 1), (6, 3))
    hand_on(2, (7, 4))
    stage_col(2)

    stage_end(1)
    first_proj = summed(1)
    basis_gram = jnp.concatenate([red_col[0, k] for k in range(8)], 0)
    writes = []

    def small_copy(n, ref):
        write = pltpu.make_async_copy(small.at[n], ref, small_sem.at[n])
        write.start()
        writes.append(write)

    coeffs = 2.0 * first_proj - exact(first_proj, basis_gram)
    left_over = first_proj - exact(coeffs, basis_gram)
    removed = exact_nt(
        jnp.concatenate([first_proj, coeffs], 1), jnp.concatenate([coeffs, left_over], 1)
    )
    small[0] = coeffs
    small_copy(0, coeffs_out)
    coeffs2 = wide(coeffs)

    def seen(k):
        chunk = basis2[:, pl.ds(pl.multiple_of(k * PIECE, PIECE), PIECE)]
        return fold(dot(coeffs2, chunk))

    def keep(k, rest):
        rest = stacked(rest)
        twice[k] = rest
        write = pltpu.make_async_copy(twice.at[k], twice_out.at[k], out_sem.at[k])
        write.start()
        writes.append(write)
        return rest

    def remove(m):
        k = col_peer(m)[0]
        if m not in (2, 4):
            for h in range(2):
                spread_wait(h, k)
        keep(k, product[k] - foreseen[k])

    def foresee(*ms):
        for m in ms:
            foreseen[col_peer(m)[0]] = seen(col_peer(m)[0])

    keep(col, product[col] - seen(col))
    foresee(1, 3, 4, 2, 5, 7, 6)
    for m in (1, 3, 4, 2):
        remove(m)
    stage_end(2)

    lane = lax.broadcasted_iota(jnp.int32, (S, 128), 1)
    line = lax.broadcasted_iota(jnp.int32, (S, 128), 0)
    gram = summed(2) - jnp.concatenate([removed, jnp.zeros((S, 128 - S), f32)], 1)
    work = jnp.where(lane == line + S, 1.0, gram)
    factor = jnp.zeros((S, 128), f32)
    scale = jnp.zeros((S, 128), f32)
    for j in range(S):
        column = jnp.broadcast_to(work[:, j:j + 1], (S, 128))
        pivot = jnp.broadcast_to(column[j:j + 1, :], (S, 128))
        root = lax.rsqrt(pivot)
        factor = jnp.where((lane == j) & (line >= j), column * root, factor)
        scale = jnp.where(line == j, root, scale)
        ratio = jnp.where(line > j, column / pivot, 0.0)
        work = work - ratio * jnp.broadcast_to(work[j:j + 1, :], (S, 128))
    small[1] = factor
    small[2] = work * scale
    small_copy(1, factor_out)
    small_copy(2, inverse_out)

    for m in (5, 7, 6):
        remove(m)

    for copy in sends:
        copy.wait_send()
    for m in range(1, 8):
        sum_copy(inbox.at[m], m, 1, 0).wait_send()
    for write in writes:
        write.wait()


def finish(
    twice_in, coeffs_in, factor_in, inverse_in, out, coeffs_out, factor_out,
    twice, final, small, corner, in_sem, out_sem, small_sem,
):
    load_small = [
        pltpu.make_async_copy(inverse_in, small.at[0], small_sem.at[0]),
        pltpu.make_async_copy(factor_in, small.at[1], small_sem.at[1]),
    ]
    loads = [pltpu.make_async_copy(twice_in.at[k], twice.at[k], in_sem.at[k]) for k in range(8)]
    writes = [pltpu.make_async_copy(coeffs_in, coeffs_out, small_sem.at[2])]
    for copy in load_small + loads + writes:
        copy.start()
    load_small[0].wait()
    inverse2 = wide(small[0][:, S:2 * S])
    for k in range(8):
        loads[k].wait()
        final[k] = fold(dot(inverse2, twice[k]))
        write = pltpu.make_async_copy(final.at[k], out.at[:, pl.ds(k * PIECE, PIECE)], out_sem.at[k])
        write.start()
        writes.append(write)
        if k == 0:
            load_small[1].wait()
            corner[...] = small[1][:, :S]
            write = pltpu.make_async_copy(corner, factor_out, small_sem.at[3])
            write.start()
            writes.append(write)
    for write in writes:
        write.wait()


def body(blocks, columns, counts, old_basis, vectors):
    bands = blocks.reshape(ROWS // BAND, BAND, SLOT, 32, 128).transpose(2, 0, 3, 1, 4)
    bands = bands.reshape(SLOT, ROWS // BAND, 32 * BAND, 128)
    D = pltpu.SemaphoreType.DMA
    V = pltpu.VMEM
    any_space = pl.BlockSpec(memory_space=pl.ANY)
    twice, coeffs, factor, inverse = pl.pallas_call(
        kernel,
        out_shape=(
            jax.ShapeDtypeStruct((8, 2 * S, PIECE), bf16),
            jax.ShapeDtypeStruct((S, KS), f32),
            jax.ShapeDtypeStruct((S, 128), f32),
            jax.ShapeDtypeStruct((S, 128), f32),
        ),
        in_specs=[any_space] * 5,
        out_specs=(any_space,) * 4,
        scratch_shapes=[
            pltpu.SMEM((SLOT, ROWS), jnp.int32),
            pltpu.SMEM((1, ROWS), jnp.int32),
            V((3, S, 128), f32),
            V((SLOT, ROWS // BAND, 32 * BAND, 128), f32),
            V((ROWS, 192, 128), bf16),
            V((ZERO_BLOCK + 1, 64, 128), bf16),
            V((128, 512), bf16),
            V((2, KS, PIECE), f32),
            V((2 * KS, UNK), bf16),
            V((2, 16, S // 2, PIECE), f32),
            V((8, S, PIECE), f32),
            V((8, S, PIECE), f32),
            V((2, S, PIECE), f32),
            V((8, S, PIECE), f32),
            V((8, S, PIECE), f32),
            V((8, 2 * S, PIECE), bf16),
            V((3, 1, S, 128), f32),
            V((3, S, 128), f32),
            V((3, 8, S, 128), f32),
            V((3, 8, S, 128), f32),
            D((2,)), D((3,)), D((SLOT,)), D((2,)), D((2,)), D((8,)),
            D((2, 18)), D((2, 16)), D((8,)), D((8,)), D((2, 8)), D((2, 8)),
            D((3,)), D((3,)), D((3, 8)), D((3, 8)), D((3, 8)), D((3, 8)),
        ],
        compiler_params=pltpu.CompilerParams(
            collective_id=0, has_side_effects=True, vmem_limit_bytes=62 << 20
        ),
    )(columns.T, counts.T, bands, vectors, old_basis)
    new_block, coeffs, factor = pl.pallas_call(
        finish,
        out_shape=(
            jax.ShapeDtypeStruct((S, UNK), f32),
            jax.ShapeDtypeStruct((S, KS), f32),
            jax.ShapeDtypeStruct((S, S), f32),
        ),
        in_specs=[any_space] * 4,
        out_specs=(any_space, any_space, any_space),
        scratch_shapes=[
            V((8, 2 * S, PIECE), bf16), V((8, S, PIECE), f32), V((2, S, 128), f32), V((S, S), f32),
            D((8,)), D((8,)), D((4,)),
        ],
        compiler_params=pltpu.CompilerParams(vmem_limit_bytes=62 << 20),
    )(twice, coeffs, factor, inverse)
    return new_block, coeffs.T, factor


def solution(mesh):
    return jax.shard_map(
        body,
        mesh=mesh,
        in_specs=(
            P("row", "col", None),
            P("row", "col"),
            P("row", "col"),
            P(None, "row"),
            P(None, "row"),
        ),
        out_specs=(P(None, "row"), P(), P()),
        check_vma=False,
    )
```

```python
import functools

import jax
import jax.numpy as jnp
from jax import lax
from jax.experimental import pallas as pl
from jax.experimental.pallas import tpu as pltpu
from jax.sharding import PartitionSpec as P

f32 = jnp.float32
bf16 = jnp.bfloat16
MESH = pl.DeviceIdType.MESH

B = 64
S = 16
SLOT = 3
BAND = 8
ROWS = 256
PIECE = 2048
UNK = 16384
KS = 128
TOTAL = 262144
ZERO_BLOCK = 512


def split(x):
    hi = x.astype(bf16)
    return hi, (x - hi.astype(f32)).astype(bf16)


def stacked(x):
    hi, lo = split(x)
    return jnp.concatenate([hi, lo], 0)


def fold(x):
    return x[:S] + x[S:]


def wide(x):
    two = stacked(x)
    return jnp.concatenate([two, two], 1)


def dot(a, b):
    return jnp.dot(a, b, preferred_element_type=f32)


def dot_nt(a, b):
    return lax.dot_general(a, b, (((1,), (1,)), ((), ())), preferred_element_type=f32)


def exact(a, b):
    return jnp.dot(a, b, precision=lax.Precision.HIGHEST, preferred_element_type=f32)


def exact_nt(a, b):
    return lax.dot_general(
        a, b, (((1,), (1,)), ((), ())), precision=lax.Precision.HIGHEST, preferred_element_type=f32
    )


def kernel(
    columns_in, counts_in, blocks, vectors, basis,
    twice_out, coeffs_out, factor_out, inverse_out,
    columns, counts, small, stage, weights, grid, expand, basis_stage, basis2, pieces, partial, inbox, relay, foreseen, product, twice,
    red_src, red_sib, red_row, red_col,
    index_sem, small_sem, load_sem, basis_sem, own_sem, out_sem,
    s1, r1, s2, r2, s3, r3, sib_s, sib_r, row_s, row_r, col_s, col_r,
):
    row = lax.axis_index("row")
    col = lax.axis_index("col")
    yh, x, core = row // 8, row // 2 % 4, row % 2
    yl, z = col // 4, col % 4
    chip = yh * 4 + x
    sibling = (row + 1 - 2 * core, col)

    def row_peer(m):
        c = (yh + m // 4) % 2 * 4 + (x + m % 4) % 4
        return c, (c * 2 + core, col)

    def col_peer(m):
        k = (yl + m // 4) % 2 * 4 + (z + m % 4) % 4
        return k, (row, k)

    barrier = pltpu.get_barrier_semaphore()
    peers = [sibling] + [row_peer(m)[1] for m in range(1, 8)] + [col_peer(m)[1] for m in range(1, 8)]
    for peer in peers:
        pl.semaphore_signal(barrier, inc=1, device_id=peer, device_id_type=MESH)

    index_loads = [
        pltpu.make_async_copy(columns_in, columns, index_sem.at[0]),
        pltpu.make_async_copy(counts_in, counts, index_sem.at[1]),
    ]
    for load in index_loads:
        load.start()
    own_loads = []
    for h in range(2):
        own_loads.append(
            pltpu.make_async_copy(
                vectors.at[8 * h:8 * h + 8, pl.ds(pl.multiple_of(col * PIECE, PIECE), PIECE)],
                pieces.at[h, row],
                own_sem.at[h],
            )
        )
        own_loads[h].start()
    loads = []
    for s in range(SLOT):
        load = pltpu.make_async_copy(blocks.at[s], stage.at[s], load_sem.at[s])
        load.start()
        loads.append(load)

    def basis_load(c):
        return pltpu.make_async_copy(
            basis.at[:, pl.ds(c * PIECE, PIECE)], basis_stage.at[c % 2], basis_sem.at[c % 2]
        )

    basis_load(0).start()
    basis_load(1).start()

    cell = lax.broadcasted_iota(jnp.int32, (128, 512), 0)
    spot = lax.broadcasted_iota(jnp.int32, (128, 512), 1)
    expand[...] = jnp.where(
        cell == spot // 256 * 64 + spot % 32 * 2 + spot // 128 % 2, 1.0, 0.0
    ).astype(bf16)
    grid[ZERO_BLOCK] = jnp.zeros((64, 128), bf16)

    for s in range(SLOT):
        loads[s].wait()

        @pl.loop(0, ROWS // BAND)
        def _(band, s=s):
            for i in range(BAND):
                hi, lo = split(stage[s, band, pl.ds(i, 32, stride=BAND), :])
                weights[band * BAND + i, 32 * s:32 * s + 32, :] = hi
                weights[band * BAND + i, 96 + 32 * s:128 + 32 * s, :] = lo

    pl.semaphore_wait(barrier, len(peers))
    for load in index_loads:
        load.wait()

    sends = []

    def send(src, dst, ssem, rsem, peer):
        copy = pltpu.make_async_remote_copy(src, dst, ssem, rsem, device_id=peer, device_id_type=MESH)
        copy.start()
        sends.append(copy)

    def arrival(dst, ssem, rsem):
        return pltpu.make_async_remote_copy(dst, dst, ssem, rsem, device_id=sibling, device_id_type=MESH)

    def pass_on(h, r, n, peer):
        send(pieces.at[h, r], pieces.at[h, r], s1.at[h, n], r1.at[h, r], peer)

    for h in range(2):
        own_loads[h].wait()
        for m in (4, 2):
            pass_on(h, row, m, row_peer(m)[1])
    for h in range(2):
        for m in (1, 3):
            pass_on(h, row, m, row_peer(m)[1])
        pass_on(h, row, 0, sibling)

    def take(h, m):
        r = row_peer(m)[0] * 2 + core
        arrival(pieces.at[h, r], s1.at[h, 0], r1.at[h, r]).wait_recv()
        if m == 4:
            pass_on(h, r, 8, row_peer(1)[1])
            pass_on(h, r, 9, row_peer(3)[1])
        if m == 2:
            pass_on(h, r, 10, row_peer(4)[1])
        pass_on(h, r, 10 + m, sibling)

    def take_sibling(h, m):
        r = row_peer(m)[0] * 2 + 1 - core
        arrival(pieces.at[h, r], s1.at[h, 0], r1.at[h, r]).wait_recv()

    own_basis = pl.multiple_of(col * 16, 16)
    gram_rows = jnp.zeros((2 * S, 2 * KS), f32)
    for c in range(8):
        basis_load(c).wait()
        chunk = stacked(basis_stage[c % 2])
        basis2[:, c * PIECE:(c + 1) * PIECE] = chunk
        if c + 2 < 8:
            basis_load(c + 2).start()
        left = jnp.concatenate(
            [
                basis2[pl.ds(own_basis, 16), c * PIECE:(c + 1) * PIECE],
                basis2[pl.ds(KS + own_basis, 16), c * PIECE:(c + 1) * PIECE],
            ],
            0,
        )
        gram_rows += dot_nt(left, chunk)

    def stage_sib(n, value):
        red_src[n, 0] = value
        send(red_src.at[n, 0], red_sib.at[n], sib_s.at[n], sib_r.at[n], sibling)

    def stage_row(n):
        arrival(red_sib.at[n], sib_s.at[n], sib_r.at[n]).wait_recv()
        red_row[n, chip] = red_src[n, 0] + red_sib[n]
        for m in range(1, 8):
            send(red_row.at[n, chip], red_row.at[n, chip], row_s.at[n, m], row_r.at[n, chip], row_peer(m)[1])

    def stage_col(n):
        for m in range(1, 8):
            c = row_peer(m)[0]
            arrival(red_row.at[n, c], row_s.at[n, m], row_r.at[n, c]).wait_recv()
        total = red_row[n, 0]
        for c in range(1, 8):
            total += red_row[n, c]
        red_col[n, col] = total * (1.0 / TOTAL)
        for m in range(1, 8):
            send(red_col.at[n, col], red_col.at[n, col], col_s.at[n, m], col_r.at[n, col], col_peer(m)[1])

    def stage_end(n):
        for m in range(1, 8):
            k = col_peer(m)[0]
            arrival(red_col.at[n, k], col_s.at[n, m], col_r.at[n, k]).wait_recv()

    def summed(n):
        total = red_col[n, 0]
        for k in range(1, 8):
            total += red_col[n, k]
        return total

    both = gram_rows[:, :KS] + gram_rows[:, KS:]
    stage_sib(0, fold(both))
    stage_row(0)

    def prepare(r):
        two = stacked(jnp.concatenate([pieces[0, r], pieces[1, r]], 0))
        for h in range(4):
            left = jnp.concatenate([two[:, 128 * u:128 * u + 128] for u in range(4 * h, 4 * h + 4)], 0)
            spread = dot(left, expand[...]).astype(bf16)
            for u in range(4):
                for q in range(2):
                    for p in range(2):
                        lanes = (2 * q + p) * 128
                        grid[r * 32 + 2 * (4 * h + u) + q, 32 * p:32 * p + 32, :] = (
                            spread[32 * u:32 * u + 32, lanes:lanes + 128]
                        )

    for h in range(2):
        for m in (4, 2, 1, 3):
            take(h, m)
    prepare(row)
    for h in range(2):
        take_sibling(h, 0)
    prepare(row + 1 - 2 * core)
    for m in (4, 2, 1, 3):
        prepare(row_peer(m)[0] * 2 + core)
        for h in range(2):
            take_sibling(h, m)
        prepare(row_peer(m)[0] * 2 + 1 - core)
    for h in range(2):
        for m in (5, 7, 6):
            take(h, m)
    for m in (5, 7, 6):
        prepare(row_peer(m)[0] * 2 + core)
        for h in range(2):
            take_sibling(h, m)
        prepare(row_peer(m)[0] * 2 + 1 - core)

    low = lax.broadcasted_iota(jnp.int32, (S, 128), 1) < 64
    group = lax.broadcasted_iota(jnp.int32, (64, 128), 1) // 32

    def block_row(i):
        live = counts[0, i]
        where = []
        for t in range(SLOT):
            g = columns[t, i]
            high = lax.shift_left(lax.shift_right_logical(g, 8), 5)
            where.append(jnp.where(live > t, high + jnp.bitwise_and(g, 31), ZERO_BLOCK))
        v0, v1, v2 = [grid[w] for w in where]
        first = jnp.where(group == 1, v1, jnp.where(group == 2, v2, v0))
        second = jnp.where(group == 0, v1, v2)
        left = jnp.concatenate([first, second], 1)[:, :192]
        res = dot(left, weights[i])
        return res[0:16] + res[16:32], res[32:48] + res[48:64]

    def sum_copy(src, m, dy, dz):
        return pltpu.make_async_remote_copy(
            src, inbox.at[m], s2.at[m], r2.at[m],
            device_id=(row, (yl + dy) % 2 * 4 + (z + dz) % 4), device_id_type=MESH,
        )

    def landed(m):
        sum_copy(inbox.at[m], m, 1, 0).wait_recv()

    def turn(n):
        m = n * 0
        for place, peer in enumerate((5, 7, 6, 1, 3, 2, 4)):
            m = jnp.where(n == place, peer, m)
        return m, (yl + m // 4) % 2 * 4 + (z + m % 4) % 4

    @pl.loop(0, 8)
    def _(n):
        m, d = turn(n)
        for u in range(16):
            even0, odd0 = block_row(d * 32 + 2 * u)
            even1, odd1 = block_row(d * 32 + 2 * u + 1)
            partial[d, :, 128 * u:128 * u + 128] = jnp.where(low, even0, odd1) + pltpu.roll(
                jnp.where(low, even1, odd0), 64, 1
            )

        @pl.when(n == 2)
        def _():
            sum_copy(partial.at[d], 6, 1, 0).start()

        @pl.when((n < 5) & (n != 2))
        def _():
            sum_copy(partial.at[d], m, 0, m % 4).start()

    def project(n, proj):
        d = turn(n)[1]
        chunk = basis2[:, pl.ds(pl.multiple_of(d * PIECE, PIECE), PIECE)]
        return proj + dot_nt(stacked(partial[d]), chunk)

    proj = lax.fori_loop(0, 4, project, jnp.zeros((2 * S, 2 * KS), f32))
    landed(5)
    landed(7)
    relay[1] = partial[col_peer(4)[0]] + (inbox[5] + inbox[7])
    sum_copy(relay.at[1], 4, 1, 0).start()
    proj = lax.fori_loop(4, 6, project, proj)
    landed(6)
    relay[0] = partial[col_peer(2)[0]] + inbox[6]
    sum_copy(relay.at[0], 2, 0, 2).start()
    proj = lax.fori_loop(6, 8, project, proj)
    both = proj[:, :KS] + proj[:, KS:]
    stage_sib(1, fold(both))
    stage_col(0)
    stage_row(1)
    for m in (1, 3, 2, 4):
        landed(m)
    total = partial[col] + (inbox[1] + inbox[3]) + (inbox[2] + inbox[4])

    def spread(h, k, n, m):
        rows = pl.ds(8 * h, 8)
        send(product.at[k, rows], product.at[k, rows], s3.at[h, n], r3.at[h, k], col_peer(m)[1])

    def spread_wait(h, k):
        rows = pl.ds(8 * h, 8)
        arrival(product.at[k, rows], s3.at[h, 0], r3.at[h, k]).wait_recv()

    product[col] = total
    for m in (4, 2, 1, 3):
        for h in range(2):
            spread(h, col, m, m)
    stage_end(0)
    stage_col(1)
    own_product = stacked(total)
    quads = dot_nt(own_product, own_product)
    quads = quads[:, :S] + quads[:, S:]
    stage_sib(2, jnp.concatenate([fold(quads), jnp.zeros((S, 128 - S), f32)], 1))
    stage_row(2)

    def hand_on(m, *next_peers):
        k = col_peer(m)[0]
        for h in range(2):
            spread_wait(h, k)
            for n, peer in next_peers:
                spread(h, k, n, peer)

    hand_on(4, (5, 1), (6, 3))
    hand_on(2, (7, 4))
    stage_col(2)

    stage_end(1)
    first_proj = summed(1)
    basis_gram = jnp.concatenate([red_col[0, k] for k in range(8)], 0)
    writes = []

    def small_copy(n, ref):
        write = pltpu.make_async_copy(small.at[n], ref, small_sem.at[n])
        write.start()
        writes.append(write)

    coeffs = 2.0 * first_proj - exact(first_proj, basis_gram)
    left_over = first_proj - exact(coeffs, basis_gram)
    removed = exact_nt(
        jnp.concatenate([first_proj, coeffs], 1), jnp.concatenate([coeffs, left_over], 1)
    )
    small[0] = coeffs
    small_copy(0, coeffs_out)
    coeffs2 = wide(coeffs)

    def seen(k):
        chunk = basis2[:, pl.ds(pl.multiple_of(k * PIECE, PIECE), PIECE)]
        return fold(dot(coeffs2, chunk))

    def keep(k, rest):
        rest = stacked(rest)
        twice[k] = rest
        write = pltpu.make_async_copy(twice.at[k], twice_out.at[k], out_sem.at[k])
        write.start()
        writes.append(write)
        return rest

    def remove(m):
        k = col_peer(m)[0]
        if m not in (2, 4):
            for h in range(2):
                spread_wait(h, k)
        keep(k, product[k] - foreseen[k])

    def foresee(*ms):
        for m in ms:
            foreseen[col_peer(m)[0]] = seen(col_peer(m)[0])

    keep(col, product[col] - seen(col))
    foresee(1, 3, 4, 2, 5, 7, 6)
    for m in (1, 3, 4, 2):
        remove(m)
    stage_end(2)

    lane = lax.broadcasted_iota(jnp.int32, (S, 128), 1)
    line = lax.broadcasted_iota(jnp.int32, (S, 128), 0)
    gram = summed(2) - jnp.concatenate([removed, jnp.zeros((S, 128 - S), f32)], 1)
    work = jnp.where(lane == line + S, 1.0, gram)
    factor = jnp.zeros((S, 128), f32)
    scale = jnp.zeros((S, 128), f32)
    for j in range(S):
        column = jnp.broadcast_to(work[:, j:j + 1], (S, 128))
        pivot = jnp.broadcast_to(column[j:j + 1, :], (S, 128))
        root = lax.rsqrt(pivot)
        factor = jnp.where((lane == j) & (line >= j), column * root, factor)
        scale = jnp.where(line == j, root, scale)
        ratio = jnp.where(line > j, column / pivot, 0.0)
        work = work - ratio * jnp.broadcast_to(work[j:j + 1, :], (S, 128))
    small[1] = factor
    small[2] = work * scale
    small_copy(1, factor_out)
    small_copy(2, inverse_out)

    for m in (5, 7, 6):
        remove(m)

    for copy in sends:
        copy.wait_send()
    for m in range(1, 8):
        sum_copy(inbox.at[m], m, 1, 0).wait_send()
    for write in writes:
        write.wait()


def finish(
    twice_in, coeffs_in, factor_in, inverse_in, out, coeffs_out, factor_out,
    twice, final, small, corner, in_sem, out_sem, small_sem,
):
    load_small = [
        pltpu.make_async_copy(inverse_in, small.at[0], small_sem.at[0]),
        pltpu.make_async_copy(factor_in, small.at[1], small_sem.at[1]),
    ]
    loads = [pltpu.make_async_copy(twice_in.at[k], twice.at[k], in_sem.at[k]) for k in range(8)]
    writes = [pltpu.make_async_copy(coeffs_in, coeffs_out, small_sem.at[2])]
    for copy in load_small + loads + writes:
        copy.start()
    load_small[0].wait()
    inverse2 = wide(small[0][:, S:2 * S])
    for k in range(8):
        loads[k].wait()
        final[k] = fold(dot(inverse2, twice[k]))
        write = pltpu.make_async_copy(final.at[k], out.at[:, pl.ds(k * PIECE, PIECE)], out_sem.at[k])
        write.start()
        writes.append(write)
        if k == 0:
            load_small[1].wait()
            corner[...] = small[1][:, :S]
            write = pltpu.make_async_copy(corner, factor_out, small_sem.at[3])
            write.start()
            writes.append(write)
    for write in writes:
        write.wait()


def body(blocks, columns, counts, old_basis, vectors):
    bands = blocks.reshape(ROWS // BAND, BAND, SLOT, 32, 128).transpose(2, 0, 3, 1, 4)
    bands = bands.reshape(SLOT, ROWS // BAND, 32 * BAND, 128)
    D = pltpu.SemaphoreType.DMA
    V = pltpu.VMEM
    any_space = pl.BlockSpec(memory_space=pl.ANY)
    twice, coeffs, factor, inverse = pl.pallas_call(
        kernel,
        out_shape=(
            jax.ShapeDtypeStruct((8, 2 * S, PIECE), bf16),
            jax.ShapeDtypeStruct((S, KS), f32),
            jax.ShapeDtypeStruct((S, 128), f32),
            jax.ShapeDtypeStruct((S, 128), f32),
        ),
        in_specs=[any_space] * 5,
        out_specs=(any_space,) * 4,
        scratch_shapes=[
            pltpu.SMEM((SLOT, ROWS), jnp.int32),
            pltpu.SMEM((1, ROWS), jnp.int32),
            V((3, S, 128), f32),
            V((SLOT, ROWS // BAND, 32 * BAND, 128), f32),
            V((ROWS, 192, 128), bf16),
            V((ZERO_BLOCK + 1, 64, 128), bf16),
            V((128, 512), bf16),
            V((2, KS, PIECE), f32),
            V((2 * KS, UNK), bf16),
            V((2, 16, S // 2, PIECE), f32),
            V((8, S, PIECE), f32),
            V((8, S, PIECE), f32),
            V((2, S, PIECE), f32),
            V((8, S, PIECE), f32),
            V((8, S, PIECE), f32),
            V((8, 2 * S, PIECE), bf16),
            V((3, 1, S, 128), f32),
            V((3, S, 128), f32),
            V((3, 8, S, 128), f32),
            V((3, 8, S, 128), f32),
            D((2,)), D((3,)), D((SLOT,)), D((2,)), D((2,)), D((8,)),
            D((2, 18)), D((2, 16)), D((8,)), D((8,)), D((2, 8)), D((2, 8)),
            D((3,)), D((3,)), D((3, 8)), D((3, 8)), D((3, 8)), D((3, 8)),
        ],
        compiler_params=pltpu.CompilerParams(
            collective_id=0, has_side_effects=True, vmem_limit_bytes=62 << 20
        ),
    )(columns.T, counts.T, bands, vectors, old_basis)
    new_block, coeffs, factor = pl.pallas_call(
        finish,
        out_shape=(
            jax.ShapeDtypeStruct((S, UNK), f32),
            jax.ShapeDtypeStruct((S, KS), f32),
            jax.ShapeDtypeStruct((S, S), f32),
        ),
        in_specs=[any_space] * 4,
        out_specs=(any_space, any_space, any_space),
        scratch_shapes=[
            V((8, 2 * S, PIECE), bf16), V((8, S, PIECE), f32), V((2, S, 128), f32), V((S, S), f32),
            D((8,)), D((8,)), D((4,)),
        ],
        compiler_params=pltpu.CompilerParams(vmem_limit_bytes=62 << 20),
    )(twice, coeffs, factor, inverse)
    return new_block, coeffs.T, factor


def solution(mesh):
    return jax.shard_map(
        body,
        mesh=mesh,
        in_specs=(
            P("row", "col", None),
            P("row", "col"),
            P("row", "col"),
            P(None, "row"),
            P(None, "row"),
        ),
        out_specs=(P(None, "row"), P(), P()),
        check_vma=False,
    )
```
